256 devices in a mesh: dp: 64 (over z_hi, x, y, core), pipe: 4 (over z_lo).
Axes of the slice: x: 4, y: 4, z: 8 (z_hi: 2, z_lo: 4; z = z_hi * 4 + z_lo), core: 2. Of those that a mesh axis runs over, the one named last changes fastest.
Arguments:
- fwd_x: bfloat16 [4, 64, 64, 3584], P('pipe', 'dp'), may hold values from -6 to 6
- fwd_q: bfloat16 [4, 64, 64, 3584], P('pipe', 'dp')
- bwd_x: bfloat16 [4, 64, 64, 3584], P('pipe', 'dp'), may hold values from -16 to 16
- bwd_q: bfloat16 [4, 64, 64, 3584], P('pipe', 'dp')
- bwd_dout: bfloat16 [4, 64, 64, 3584], P('pipe', 'dp'), may hold values from -6 to 6
- cache_kv: bfloat16 [4, 64, 1024, 1024], P('pipe', 'dp'), may hold values from -6 to 6
- kv_weight: bfloat16 [4, 3584, 1024], P('pipe', 'dp'), may hold values from -0.09375 to 0.09375
- seg_lengths: int32 [4, 64, 4], P('pipe', 'dp'), may hold values from 1 to 896, as said below
Outputs:
- next_act: bfloat16 [4, 64, 64, 3584], P('pipe', 'dp')
- grad_q: bfloat16 [4, 64, 64, 3584], P('pipe', 'dp')
- prev_grad: bfloat16 [4, 64, 64, 3584], P('pipe', 'dp')
- weight_grad: float32 [4, 3584, 1024], P('pipe', 'dp')
The draws below stay inside these ranges and needn't reach their ends.
Inputs may be any that keep to these rules, and one draw needn't show every extreme that they name: `seg_lengths`: each row holds four lengths that sum to 1024; the first is at least 1; the second lies from 64 to 127 and is 64 in some row of every draw; the third is at most 64 and equals 64 in some row of every draw; the fourth lies from 32 to the third.
All inputs are finite; a program needn't handle non-finite values.
Results may differ from the reference program's by a relative error of at most 0.035.
Values may be sent and summed in bfloat16 or wider, within the bound.
No kernel may reach another device: no remote copies, remote signals or barrier semaphores. Data moves between devices by JAX's collectives and lax.ppermute only.
A program may use at most 128 MiB of HBM per device.

```python
import math
import jax
import jax.numpy as jnp
from jax import lax

D = 3584
HQ = 28
HK = 4
HD = 128
SEG = 64
SEQ = 1024
SECTIONS = 4
SEQS = 64


def cache_base(key):
    base = jax.random.normal(key, (SECTIONS, SEQS, SEQ, 2 * HK * HD), jnp.float32)
    return jnp.clip(base, -6.0, 6.0)


def draw_cache_kv(key, part):
    base = cache_base(key)
    return base.astype(jnp.bfloat16)


def draw_fwd_q(key, part):
    key = jax.random.fold_in(key, 11)
    query = jnp.clip(jax.random.normal(key, (SECTIONS, SEQS, SEG, HQ * HD), jnp.float32), -6.0, 6.0)
    return query.astype(jnp.bfloat16)


def draw_bwd_q(key, part):
    key = jax.random.fold_in(key, 13)
    query = jnp.clip(jax.random.normal(key, (SECTIONS, SEQS, SEG, HQ * HD), jnp.float32), -6.0, 6.0)
    return query.astype(jnp.bfloat16)


def draw_seg_lengths(key, part):
    key = jax.random.fold_in(key, 5)
    key_third, key_pick, key_fourth, key_second = jax.random.split(key, 4)
    shape = (SECTIONS, SEQS)
    count = SECTIONS * SEQS
    third = jax.random.randint(key_third, shape, SEG // 2, SEG + 1)
    pick = jax.random.randint(key_pick, (), 0, count)
    other = (pick + 1) % count
    flat_index = jnp.arange(count, dtype=jnp.int32).reshape(shape)
    is_pick = flat_index == pick
    is_other = flat_index == other
    third = jnp.where(is_pick, SEG, third)
    third = jnp.where(is_other, SEG // 2, third)
    spread = jax.random.randint(key_fourth, shape, 0, 1 << 20)
    fourth = SEG // 2 + spread % (third - SEG // 2 + 1)
    fourth = jnp.where(is_pick | is_other, SEG // 2, fourth)
    second = jax.random.randint(key_second, shape, SEG, 2 * SEG)
    second = jnp.where(is_other, SEG, second)
    first = SEQ - second - third - fourth
    return jnp.stack([first, second, third, fourth], axis=-1).astype(jnp.int32)


def spiked(drawn, rng, source, target, shards_of, factor):
    def block_of(axis_at):
        return (jnp.arange(drawn.shape[axis_at]) // (drawn.shape[axis_at] // shards_of)).reshape((-1,) + (1,) * (drawn.ndim - 1 - axis_at))

    first = jax.random.permutation(rng, shards_of)[block_of(target)]
    far = (block_of(target) + shards_of // 2) % shards_of
    return jnp.where((block_of(source) == first) | (block_of(source) == far), factor * drawn, drawn)


def block_levels(key, shape, cuts, smallest, top_value):
    loudness = 1.0
    for position, shards_of in cuts:
        heights = jax.random.uniform(jax.random.fold_in(jax.random.fold_in(key, 6), position), (shards_of,), jnp.float32, smallest / len(cuts), top_value / len(cuts))
        loudness = loudness * jnp.repeat(jnp.exp(heights), shape[position] // shards_of).reshape((-1,) + (1,) * (len(shape) - 1 - position))
    return loudness


def noise(rng, shape, width, reach, cuts=(), kind=jnp.bfloat16):
    entries = width * jax.random.normal(rng, shape, jnp.float32)
    if cuts:
        entries = entries * block_levels(rng, shape, cuts, -0.22, 0.18)
    return jnp.clip(entries, -reach, reach).astype(kind)


def gaussian_with(rng, shape, scale, reach, shards, heavy, held_as=jnp.bfloat16):
    values = scale * jax.random.normal(rng, shape, jnp.float32)
    if shards:
        values = values * block_levels(rng, shape, shards, -0.22, 0.18)
    return jnp.clip(spiked(values, jax.random.fold_in(rng, 3), *heavy), -reach, reach).astype(held_as)


def setup_inputs(seed: int = 0) -> dict:
    splits = jax.random.split(jax.random.key(seed), 9)
    fwd_x = noise(splits[0], (SECTIONS, SEQS, SEG, D), 1.0, 6.0, ((0, 4), (1, 64)))
    fwd_q = draw_fwd_q(jax.random.fold_in(splits[8], 71), 0)
    bwd_x = gaussian_with(splits[2], (SECTIONS, SEQS, SEG, D), 1.0, 16.0, ((0, 4), (1, 64)), (1, 3, 64, 4.0))
    bwd_q = draw_bwd_q(jax.random.fold_in(splits[8], 71), 0)
    bwd_dout = noise(splits[4], (SECTIONS, SEQS, SEG, HQ * HD), 1.0, 6.0, ((0, 4), (1, 64)))
    cache_kv = draw_cache_kv(jax.random.fold_in(splits[8], 71), 0)
    kv_weight = noise(splits[6], (SECTIONS, D, 2 * HK * HD), D ** -0.5, 0.09375, ((0, 4), (1, 64)))
    seg_lengths = draw_seg_lengths(jax.random.fold_in(splits[8], 71), 0)
    return {"fwd_x": fwd_x, "fwd_q": fwd_q, "bwd_x": bwd_x, "bwd_q": bwd_q, "bwd_dout": bwd_dout, "cache_kv": cache_kv, "kv_weight": kv_weight, "seg_lengths": seg_lengths}


def masked_softmax(scores, allowed):
    masked = jnp.where(allowed[:, None, :], scores, -1e+30)
    top = lax.optimization_barrier(jnp.max(masked, axis=-1, keepdims=True))
    raised = jnp.exp(masked - top)
    return raised / lax.optimization_barrier(jnp.sum(raised, axis=-1, keepdims=True))

def forward_segment(query, own_kv, cache, length):
    seg = query.shape[0]
    seq_len = cache.shape[0]
    half = cache.shape[1] // 2
    kv_heads = half // HD
    group = query.shape[1] // half
    scale = 1.0 / math.sqrt(HD)
    start = (seq_len - length).astype(jnp.int32)
    rows = jnp.arange(seg, dtype=jnp.int32)
    cache_ok = jnp.broadcast_to(jnp.arange(seq_len, dtype=jnp.int32)[None, :] < start, (seg, seq_len))
    own_ok = (rows[None, :] <= rows[:, None]) & (rows[None, :] < length)
    allowed = jnp.concatenate([cache_ok, own_ok], axis=1)
    keys = jnp.concatenate([cache[:, :half], own_kv[:, :half]], axis=0)
    values = jnp.concatenate([cache[:, half:], own_kv[:, half:]], axis=0)
    pieces = []
    for head in range(kv_heads):
        block = query[:, head * group * HD:(head + 1) * group * HD].reshape(seg * group, HD)
        key_head = keys[:, head * HD:(head + 1) * HD]
        scores = (jnp.dot(block, key_head.T, preferred_element_type=jnp.float32) * scale).reshape(seg, group, -1)
        probs = masked_softmax(scores, allowed).astype(jnp.bfloat16).reshape(seg * group, -1)
        mixed = jnp.dot(probs, values[:, head * HD:(head + 1) * HD], preferred_element_type=jnp.float32)
        pieces.append(mixed.reshape(seg, group * HD))
    result = jnp.concatenate(pieces, axis=1)
    return jnp.where((rows < length)[:, None], result, 0.0).astype(jnp.bfloat16)

def backward_segment(query, dout, cache, third, fourth):
    seg = query.shape[0]
    seq_len = cache.shape[0]
    half = cache.shape[1] // 2
    kv_heads = half // HD
    group = query.shape[1] // half
    scale = 1.0 / math.sqrt(HD)
    start = (seq_len - fourth - third).astype(jnp.int32)
    rows = jnp.arange(seg, dtype=jnp.int32)
    allowed = jnp.arange(seq_len, dtype=jnp.int32)[None, :] <= start + rows[:, None]
    live = (rows < third)[:, None]
    dout = jnp.where(live, dout, jnp.zeros_like(dout))
    query_parts, key_parts, value_parts = ([], [], [])
    for head in range(kv_heads):
        block = query[:, head * group * HD:(head + 1) * group * HD].reshape(seg * group, HD)
        grad_block = dout[:, head * group * HD:(head + 1) * group * HD].reshape(seg * group, HD)
        key_head = cache[:, head * HD:(head + 1) * HD]
        value_head = cache[:, half + head * HD:half + (head + 1) * HD]
        scores = (jnp.dot(block, key_head.T, preferred_element_type=jnp.float32) * scale).reshape(seg, group, seq_len)
        probs = masked_softmax(scores, allowed).reshape(seg * group, seq_len)
        rounded = probs.astype(jnp.bfloat16)
        mixed = jnp.dot(rounded, value_head, preferred_element_type=jnp.float32)
        delta = lax.optimization_barrier(jnp.sum(grad_block.astype(jnp.float32) * mixed, axis=1, keepdims=True))
        along = jnp.dot(grad_block, value_head.T, preferred_element_type=jnp.float32)
        dscore = (probs * (along - delta)).astype(jnp.bfloat16)
        query_parts.append((jnp.dot(dscore, key_head, preferred_element_type=jnp.float32) * scale).reshape(seg, group * HD))
        dscore_own = lax.dynamic_slice_in_dim(dscore, start, seg, 1)
        rounded_own = lax.dynamic_slice_in_dim(rounded, start, seg, 1)
        key_parts.append(jnp.dot(dscore_own.T, block, preferred_element_type=jnp.float32) * scale)
        value_parts.append(jnp.dot(rounded_own.T, grad_block, preferred_element_type=jnp.float32))
    grad_query = jnp.concatenate(query_parts, axis=1).astype(jnp.bfloat16)
    kv_grad = jnp.concatenate(key_parts + value_parts, axis=1)
    kv_grad = jnp.where(live, kv_grad, 0.0).astype(jnp.bfloat16)
    return (grad_query, kv_grad)

def reference(fwd_x, fwd_q, bwd_x, bwd_q, bwd_dout, cache_kv, kv_weight, seg_lengths):

    def section(items):
        section_fx, section_fq, section_bx, section_bq, section_dout, section_cache, weight, section_lengths = items

        def one(total, item):
            fx_seq, fq_seq, bx_seq, bq_seq, dout_seq, cache_seq, lengths_seq = item
            own_kv = jnp.dot(fx_seq, weight, preferred_element_type=jnp.float32).astype(jnp.bfloat16)
            fwd_out = forward_segment(fq_seq, own_kv, cache_seq, lengths_seq[3])
            grad_query, kv_grad = backward_segment(bq_seq, dout_seq, cache_seq, lengths_seq[2], lengths_seq[3])
            input_grad = jnp.dot(kv_grad, weight.T, preferred_element_type=jnp.float32).astype(jnp.bfloat16)
            total = total + jnp.dot(bx_seq.T, kv_grad, preferred_element_type=jnp.float32)
            return (total, (fwd_out, grad_query, input_grad))
        empty = jnp.zeros((weight.shape[0], weight.shape[1]), jnp.float32)
        return lax.scan(one, empty, (section_fx, section_fq, section_bx, section_bq, section_dout, section_cache, section_lengths))
    weight_grad, (fwd_out, grad_q, input_grad) = lax.map(section, (fwd_x, fwd_q, bwd_x, bwd_q, bwd_dout, cache_kv, kv_weight, seg_lengths))
    next_act = jnp.concatenate([jnp.zeros_like(fwd_out[:1]), fwd_out[:-1]], axis=0)
    prev_grad = jnp.concatenate([input_grad[1:], jnp.zeros_like(input_grad[:1])], axis=0)
    return (next_act, grad_q, prev_grad, weight_grad)
```

```python
import functools
import math

import jax
import jax.numpy as jnp
from jax import lax
from jax.experimental import pallas as pl
from jax.experimental.pallas import tpu as pltpu
from jax.sharding import PartitionSpec as P

HD = 128
GROUP = 7
SEG = 64
BLK = 56
ROWS = GROUP * SEG
WIDE = GROUP * HD
SCALE = 1.0 / math.sqrt(HD)
EXP_SCALE = SCALE * math.log2(math.e)
F32 = jnp.float32
BF16 = jnp.bfloat16
VMEM_LIMIT = 48 * 1024 * 1024


def params():
    return pltpu.CompilerParams(vmem_limit_bytes=VMEM_LIMIT)


def cost(us):
    return pl.CostEstimate(
        flops=int(us * 1.0e9), bytes_accessed=int(us * 1.0e6), transcendentals=0
    )


def dp_target(d, z=0, x=0, y=0, c=0):
    cz, cx, cy, cc = d // 32, (d // 8) % 4, (d // 2) % 4, d % 2
    return ((((cz + z) % 2) * 4 + (cx + x) % 4) * 4 + (cy + y) % 4) * 2 + (cc + c) % 2


def move(value, **steps):
    return lax.ppermute(value, "dp", [(d, dp_target(d, **steps)) for d in range(64)])


def move_back_section(value, **steps):
    pairs = [
        (d * 4 + p, dp_target(d, **steps) * 4 + p - 1) for d in range(64) for p in range(1, 4)
    ]
    return lax.ppermute(value, ("dp", "pipe"), pairs)


def block_index(pos_ref, x, rc, k, rz):
    z, y, c = pos_ref[0], pos_ref[2], pos_ref[3]
    return (((z ^ rz) * 4 + x) * 4 + ((y + 4 - k) & 3)) * 2 + (c ^ rc)


def piece_order():
    return [(rc, k, rz) for rc in range(2) for k in range(4) for rz in range(2)]


def split_kernel(pos_ref, fx_ref, bx_ref, o0, o1, o2, o3, scr):
    for s in range(64):
        scr[s, 0:SEG, :] = fx_ref[:, s * BLK : (s + 1) * BLK]
        scr[s, SEG : 2 * SEG, :] = bx_ref[:, s * BLK : (s + 1) * BLK]
    for dx, out in enumerate((o0, o1, o2, o3)):
        x = (pos_ref[1] + dx) & 3
        out[...] = jnp.concatenate(
            [scr[block_index(pos_ref, x, rc, k, rz)] for rc, k, rz in piece_order()], axis=1
        )


def split_inputs(pos, fx, bx):
    piece = jax.ShapeDtypeStruct((2 * SEG, 16 * BLK), BF16)
    return pl.pallas_call(
        split_kernel,
        out_shape=[piece] * 4,
        in_specs=[
            pl.BlockSpec(memory_space=pltpu.SMEM),
            pl.BlockSpec(memory_space=pltpu.VMEM),
            pl.BlockSpec(memory_space=pltpu.VMEM),
        ],
        out_specs=[pl.BlockSpec(memory_space=pltpu.VMEM)] * 4,
        scratch_shapes=[pltpu.VMEM((64, 2 * SEG, BLK), BF16)],
        compiler_params=params(),
        cost_estimate=cost(3),
        name="split_inputs",
    )(pos, fx, bx)


def join_kernel(pos_ref, g0, g1, g2, g3, out_ref, scr):
    for k0, piece in enumerate((g0, g1, g2, g3)):
        x = (pos_ref[1] + k0) & 3
        for m, (rc, k, rz) in enumerate(piece_order()):
            scr[block_index(pos_ref, x, rc, k, rz)] = piece[:, m * BLK : (m + 1) * BLK]
    out_ref[...] = jnp.concatenate([scr[s] for s in range(64)], axis=1)


def join_pieces(pos, pieces):
    return pl.pallas_call(
        join_kernel,
        out_shape=jax.ShapeDtypeStruct((SEG, 64 * BLK), BF16),
        in_specs=[pl.BlockSpec(memory_space=pltpu.SMEM)]
        + [pl.BlockSpec(memory_space=pltpu.VMEM)] * 4,
        out_specs=pl.BlockSpec(memory_space=pltpu.VMEM),
        scratch_shapes=[pltpu.VMEM((64, SEG, BLK), BF16)],
        compiler_params=params(),
        cost_estimate=cost(2),
        name="join_pieces",
    )(pos, *pieces)


def dot_nt(a, b):
    return lax.dot_general(a, b, (((1,), (1,)), ((), ())), preferred_element_type=F32)


def dot_tn(a, b):
    return lax.dot_general(a, b, (((0,), (0,)), ((), ())), preferred_element_type=F32)


def dot_nn(a, b):
    return lax.dot_general(a, b, (((1,), (0,)), ((), ())), preferred_element_type=F32)


def stack_heads(block):
    return jnp.concatenate([block[:, h * HD : (h + 1) * HD] for h in range(GROUP)], axis=0)


def unstack_heads(rows):
    return jnp.concatenate([rows[h * SEG : (h + 1) * SEG] for h in range(GROUP)], axis=1)


def row_in_segment(shape):
    return lax.broadcasted_iota(jnp.int32, shape, 0) & (SEG - 1)


def backward_kernel(len_ref, q_ref, do_ref, k_ref, v_ref, gq_ref, dk_ref, dv_ref):
    third, fourth = len_ref[2], len_ref[3]
    seq = k_ref.shape[0]
    base = seq - 2 * SEG
    offset = seq - fourth - third - base
    q = stack_heads(q_ref[...])
    live = lax.broadcasted_iota(jnp.int32, (SEG, WIDE), 0) < third
    dout = stack_heads(jnp.where(live, do_ref[...], jnp.zeros((SEG, WIDE), BF16)))
    keys = k_ref[...]
    values = v_ref[...]
    scores = dot_nt(q, keys)
    tail_at = lax.broadcasted_iota(jnp.int32, (ROWS, 2 * SEG), 1)
    tail_ok = tail_at <= offset + row_in_segment((ROWS, 2 * SEG))
    tail = jnp.where(tail_ok, scores[:, base:], -1e30)
    scores = jnp.concatenate([scores[:, :base], tail], axis=1)
    top = jnp.max(scores, axis=1, keepdims=True)
    raised = jnp.exp2((scores - top) * EXP_SCALE)
    probs = raised * (1.0 / jnp.sum(raised, axis=1, keepdims=True))
    rounded = probs.astype(BF16)
    mixed = dot_nn(rounded, values)
    delta = jnp.sum(dout.astype(F32) * mixed, axis=1, keepdims=True)
    along = dot_nt(dout, values)
    dscore = (probs * (along - delta)).astype(BF16)
    gq_ref[...] = unstack_heads((dot_nn(dscore, keys) * SCALE).astype(BF16))
    dk = dot_tn(dscore[:, base:], q) * SCALE
    dv = dot_tn(rounded[:, base:], dout)
    keep = lax.broadcasted_iota(jnp.int32, (SEG, HD), 0) < third
    shift = (2 * SEG - offset) & (2 * SEG - 1)
    dk = pltpu.roll(dk, shift, 0)[:SEG]
    dv = pltpu.roll(dv, shift, 0)[:SEG]
    dk_ref[...] = jnp.where(keep, dk, 0.0).astype(BF16)
    dv_ref[...] = jnp.where(keep, dv, 0.0).astype(BF16)


def group_specs(seq, first):
    rows = pl.BlockSpec((SEG, WIDE), lambda g: (0, g + first))
    key = pl.BlockSpec((seq, HD), lambda g: (0, g + first))
    value = pl.BlockSpec((seq, HD), lambda g: (0, g + first + 4))
    return rows, key, value


def backward_groups(lengths, q, dout, cache, first, count):
    rows, key, value = group_specs(cache.shape[0], first)
    return pl.pallas_call(
        backward_kernel,
        grid=(count,),
        out_shape=[
            jax.ShapeDtypeStruct((SEG, count * WIDE), BF16),
            jax.ShapeDtypeStruct((SEG, count * HD), BF16),
            jax.ShapeDtypeStruct((SEG, count * HD), BF16),
        ],
        in_specs=[pl.BlockSpec(memory_space=pltpu.SMEM), rows, rows, key, value],
        out_specs=[
            pl.BlockSpec((SEG, WIDE), lambda g: (0, g)),
            pl.BlockSpec((SEG, HD), lambda g: (0, g)),
            pl.BlockSpec((SEG, HD), lambda g: (0, g)),
        ],
        compiler_params=params(),
        cost_estimate=cost(4 * count),
        name="backward_groups",
    )(lengths, q, dout, cache, cache)


def stored_kernel(len_ref, q_ref, k_ref, v_ref, acc_ref, stat_ref):
    fourth = len_ref[3]
    seq = k_ref.shape[0]
    base = seq - HD
    q = stack_heads(q_ref[...])
    scores = dot_nt(q, k_ref[...])
    tail_ok = lax.broadcasted_iota(jnp.int32, (ROWS, HD), 1) < HD - fourth
    tail = jnp.where(tail_ok, scores[:, base:], -1e30)
    scores = jnp.concatenate([scores[:, :base], tail], axis=1)
    top = jnp.max(scores, axis=1, keepdims=True)
    raised = jnp.exp2((scores - top) * EXP_SCALE)
    total = jnp.sum(raised, axis=1, keepdims=True)
    acc_ref[...] = unstack_heads(dot_nn(raised.astype(BF16), v_ref[...]))
    lane = lax.broadcasted_iota(jnp.int32, (SEG, HD), 1)
    stat = jnp.zeros((SEG, HD), F32)
    for h in range(GROUP):
        stat = jnp.where(lane == h, top[h * SEG : (h + 1) * SEG], stat)
        stat = jnp.where(lane == 64 + h, total[h * SEG : (h + 1) * SEG], stat)
    stat_ref[...] = stat


def stored_groups(lengths, q, cache, first, count):
    rows, key, value = group_specs(cache.shape[0], first)
    return pl.pallas_call(
        stored_kernel,
        grid=(count,),
        out_shape=[
            jax.ShapeDtypeStruct((SEG, count * WIDE), F32),
            jax.ShapeDtypeStruct((SEG, count * HD), F32),
        ],
        in_specs=[pl.BlockSpec(memory_space=pltpu.SMEM), rows, key, value],
        out_specs=[
            pl.BlockSpec((SEG, WIDE), lambda g: (0, g)),
            pl.BlockSpec((SEG, HD), lambda g: (0, g)),
        ],
        compiler_params=params(),
        cost_estimate=cost(2 * count),
        name="stored_groups",
    )(lengths, q, cache, cache)


def own_kernel(len_ref, q_ref, k0, k1, k2, k3, v0, v1, v2, v3, acc_ref, stat_ref, out_ref):
    fourth = len_ref[3]
    keys = (k0[...] + k1[...].astype(F32) + k2[...].astype(F32) + k3[...].astype(F32)).astype(BF16)
    values = (v0[...] + v1[...].astype(F32) + v2[...].astype(F32) + v3[...].astype(F32)).astype(BF16)
    q = stack_heads(q_ref[...])
    acc = stack_heads(acc_ref[...])
    stat = stat_ref[...]
    top_c = jnp.concatenate([stat[:, h : h + 1] for h in range(GROUP)], axis=0)
    total_c = jnp.concatenate([stat[:, 64 + h : 65 + h] for h in range(GROUP)], axis=0)
    scores = dot_nt(q, keys)
    at = lax.broadcasted_iota(jnp.int32, (ROWS, SEG), 1)
    row = row_in_segment((ROWS, SEG))
    scores = jnp.where((at <= row) & (at < fourth), scores, -1e30)
    top = jnp.maximum(top_c, jnp.max(scores, axis=1, keepdims=True))
    keep = jnp.exp2((top_c - top) * EXP_SCALE)
    raised = jnp.exp2((scores - top) * EXP_SCALE)
    total = total_c * keep + jnp.sum(raised, axis=1, keepdims=True)
    mixed = acc * keep + dot_nn(raised.astype(BF16), values)
    mixed = mixed * (1.0 / total)
    mixed = jnp.where(row_in_segment((ROWS, HD)) < fourth, mixed, 0.0)
    out_ref[...] = unstack_heads(mixed.astype(BF16))


def own_groups(lengths, q, parts, acc, stat):
    rows = pl.BlockSpec((SEG, WIDE), lambda g: (0, g))
    key = pl.BlockSpec((SEG, HD), lambda g: (0, g))
    value = pl.BlockSpec((SEG, HD), lambda g: (0, g + 4))
    return pl.pallas_call(
        own_kernel,
        grid=(4,),
        out_shape=jax.ShapeDtypeStruct((SEG, 4 * WIDE), BF16),
        in_specs=[pl.BlockSpec(memory_space=pltpu.SMEM), rows]
        + [key] * 4
        + [value] * 4
        + [rows, key],
        out_specs=rows,
        compiler_params=params(),
        cost_estimate=cost(4),
        name="own_groups",
    )(lengths, q, *parts, *parts, acc, stat)


def own_kv_kernel(r0, r1, r2, r3, wn_ref, wf_ref, p0, p1, p2, p3):
    x = jnp.concatenate([r[0:SEG, :] for r in (r0, r1, r2, r3)], axis=0)
    half = 8 * BLK
    total = dot_nn(x[:, :half], wn_ref[...]) + dot_nn(x[:, half:], wf_ref[...])
    for k, out in enumerate((p0, p1, p2, p3)):
        out[...] = total[k * SEG : (k + 1) * SEG].astype(out.dtype)


def own_kv_parts(pieces, near, far):
    shape = (SEG, near.shape[1])
    return pl.pallas_call(
        own_kv_kernel,
        out_shape=[jax.ShapeDtypeStruct(shape, F32)] + [jax.ShapeDtypeStruct(shape, BF16)] * 3,
        compiler_params=params(),
        cost_estimate=cost(2),
        name="own_kv_parts",
    )(*pieces, near, far)


def weight_grad_kernel(side, r0, r1, r2, r3, g0, g1, g2, g3, out_ref):
    half = 8 * BLK
    x = jnp.concatenate(
        [r[SEG : 2 * SEG, side * half : (side + 1) * half] for r in (r0, r1, r2, r3)], axis=0
    )
    grads = jnp.concatenate([g[...] for g in (g0, g1, g2, g3)], axis=0)
    out_ref[...] = dot_tn(x, grads).astype(out_ref.dtype)


def weight_grad_half(side, pieces, grads, dtype):
    return pl.pallas_call(
        functools.partial(weight_grad_kernel, side),
        out_shape=jax.ShapeDtypeStruct((8 * BLK, grads[0].shape[1]), dtype),
        compiler_params=params(),
        cost_estimate=cost(2),
        name="weight_grad_half",
    )(*pieces, *grads)


def input_grad_kernel(g0, g1, g2, g3, wn_ref, wf_ref, o0, o1, o2, o3):
    grads = jnp.concatenate([g[...] for g in (g0, g1, g2, g3)], axis=0)
    near = dot_nt(grads, wn_ref[...]).astype(BF16)
    far = dot_nt(grads, wf_ref[...]).astype(BF16)
    both = jnp.concatenate([near, far], axis=1)
    for k, out in enumerate((o0, o1, o2, o3)):
        out[...] = both[k * SEG : (k + 1) * SEG]


def input_grad_pieces(grads, near, far):
    return pl.pallas_call(
        input_grad_kernel,
        out_shape=[jax.ShapeDtypeStruct((SEG, 16 * BLK), BF16)] * 4,
        compiler_params=params(),
        cost_estimate=cost(2),
        name="input_grad_pieces",
    )(*grads, near, far)


def shards(fwd_x, fwd_q, bwd_x, bwd_q, bwd_dout, cache_kv, kv_weight, seg_lengths):
    shard = kv_weight[0]
    lengths = seg_lengths[0, 0]
    cache = cache_kv[0, 0]
    front_q, back_q, back_dout = fwd_q[0, 0], bwd_q[0, 0], bwd_dout[0, 0]
    d = lax.axis_index("dp")
    pos = jnp.stack([d // 32, (d // 8) % 4, (d // 2) % 4, d % 2]).astype(jnp.int32)

    pair = jnp.concatenate([shard, move(shard, z=1)], axis=0)
    split = split_inputs(pos, fwd_x[0, 0], bwd_x[0, 0])
    pieces = [split[0]] + [move(split[k], x=k) for k in (1, 2, 3)]

    gq0, dk0, dv0 = backward_groups(lengths, back_q, back_dout, cache, 0, 2)
    near = jnp.concatenate([pair] + [move(pair, y=k) for k in (1, 2, 3)], axis=0)
    gq1, dk1, dv1 = backward_groups(lengths, back_q, back_dout, cache, 2, 2)
    far = move(near, c=1)
    grad_query = jnp.concatenate([gq0, gq1], axis=1)
    kv_grad = jnp.concatenate([dk0, dk1, dv0, dv1], axis=1)
    grads = [kv_grad] + [move(kv_grad, x=k) for k in (1, 2, 3)]

    own_parts = own_kv_parts(pieces, near, far)
    parts = [own_parts[0]] + [move(own_parts[k], x=-k) for k in (1, 2, 3)]
    acc, stat = stored_groups(lengths, front_q, cache, 0, 4)

    away = weight_grad_half(1, pieces, grads, BF16)
    swapped = move(away, c=1)
    home = weight_grad_half(0, pieces, grads, F32)
    backs = input_grad_pieces(grads, near, far)
    backs = [move_back_section(backs[k], x=-k) for k in range(4)]

    summed = home + swapped.astype(F32)
    rows = 2 * BLK
    held = summed[:rows]
    for k in (1, 2, 3):
        held = held + move(summed[k * rows : (k + 1) * rows].astype(BF16), y=-k).astype(F32)
    weight_grad = held[:BLK] + move(held[BLK:].astype(BF16), z=1).astype(F32)

    fwd_out = own_groups(lengths, front_q, parts, acc, stat)
    next_act = lax.ppermute(fwd_out, "pipe", [(p, p + 1) for p in range(3)])
    prev_grad = join_pieces(pos, backs)
    return (next_act[None, None], grad_query[None, None], prev_grad[None, None], weight_grad[None])


def solution(mesh):
    return jax.shard_map(
        shards,
        mesh=mesh,
        in_specs=(
            P("pipe", "dp", None, None),
            P("pipe", "dp", None, None),
            P("pipe", "dp", None, None),
            P("pipe", "dp", None, None),
            P("pipe", "dp", None, None),
            P("pipe", "dp", None, None),
            P("pipe", "dp", None),
            P("pipe", "dp", None),
        ),
        out_specs=(
            P("pipe", "dp", None, None),
            P("pipe", "dp", None, None),
            P("pipe", "dp", None, None),
            P("pipe", "dp", None),
        ),
        check_vma=False,
    )
```

```python
import functools
import math

import jax
import jax.numpy as jnp
from jax import lax
from jax.experimental import pallas as pl
from jax.experimental.pallas import tpu as pltpu
from jax.sharding import PartitionSpec as P

HD = 128
GROUP = 7
SEG = 64
BLK = 56
PART = 8 * BLK
ROWS = GROUP * SEG
WIDE = GROUP * HD
SCALE = 1.0 / math.sqrt(HD)
EXP_SCALE = SCALE * math.log2(math.e)
F32 = jnp.float32
BF16 = jnp.bfloat16
VMEM_LIMIT = 32 * 1024 * 1024
VMEM_MOST = 60 * 1024 * 1024


def params(limit=VMEM_LIMIT):
    return pltpu.CompilerParams(vmem_limit_bytes=limit)


def cost(us):
    return pl.CostEstimate(
        flops=int(us * 5.0e8), bytes_accessed=int(us * 1.0e6), transcendentals=0
    )


def partner(d, z=0, x=0, y=0, c=0):
    return d ^ (z * 32 + x * 8 + y * 2 + c)


def place():
    d = lax.axis_index("dp")
    return d >> 5, (d >> 3) & 3, (d >> 1) & 3, d & 1


def swap(value, **steps):
    return lax.ppermute(value, "dp", [(d, partner(d, **steps)) for d in range(64)])


def swap_back_section(value, **steps):
    pairs = [(d * 4 + p, partner(d, **steps) * 4 + p - 1) for d in range(64) for p in range(1, 4)]
    return lax.ppermute(value, ("dp", "pipe"), pairs)


def split_kernel(fx_hbm, bx_hbm, o0, o1, o2, o3, fx_ref, bx_ref, scr, sems):
    half = 4 * PART
    copies = []
    for i, (source, held) in enumerate(((fx_hbm, fx_ref), (bx_hbm, bx_ref))):
        for j in range(2):
            cols = pl.ds(j * half, half)
            copy = pltpu.make_async_copy(source.at[:, cols], held.at[:, cols], sems.at[2 * i + j])
            copy.start()
            copies.append(copy)
    for copy in copies:
        copy.wait()
    for s in range(8):
        scr[s, 0:SEG, :] = fx_ref[:, s * PART : (s + 1) * PART]
        scr[s, SEG : 2 * SEG, :] = bx_ref[:, s * PART : (s + 1) * PART]
    z, x, _, _ = place()
    for r, out in enumerate((o0, o1, o2, o3)):
        near = scr[z * 4 + (x ^ r)]
        far = scr[(z ^ 1) * 4 + (x ^ r)]
        out[...] = jnp.concatenate([near, far], axis=1)


def split_inputs(fx, bx):
    vmem = pl.BlockSpec(memory_space=pltpu.VMEM)
    hbm = pl.BlockSpec(memory_space=pltpu.HBM)
    return pl.pallas_call(
        split_kernel,
        out_shape=[jax.ShapeDtypeStruct((2 * SEG, 2 * PART), BF16)] * 4,
        in_specs=[hbm, hbm],
        out_specs=[vmem] * 4,
        scratch_shapes=[
            pltpu.VMEM((SEG, 8 * PART), BF16),
            pltpu.VMEM((SEG, 8 * PART), BF16),
            pltpu.VMEM((8, 2 * SEG, PART), BF16),
            pltpu.SemaphoreType.DMA((4,)),
        ],
        compiler_params=params(VMEM_MOST),
        cost_estimate=cost(1.5),
        name="split_inputs",
    )(fx, bx)


def join_kernel(g03, g12, out_ref, scr):
    z, x, _, _ = place()
    for r, (piece, at) in enumerate(((g03, 0), (g12, 0), (g12, SEG), (g03, SEG))):
        scr[z * 4 + (x ^ r)] = piece[at : at + SEG, :PART]
        scr[(z ^ 1) * 4 + (x ^ r)] = piece[at : at + SEG, PART:]
    out_ref[...] = jnp.concatenate([scr[s] for s in range(8)], axis=1)


def join_pieces(g03, g12):
    vmem = pl.BlockSpec(memory_space=pltpu.VMEM)
    return pl.pallas_call(
        join_kernel,
        out_shape=jax.ShapeDtypeStruct((SEG, 8 * PART), BF16),
        in_specs=[vmem, vmem],
        out_specs=vmem,
        scratch_shapes=[pltpu.VMEM((8, SEG, PART), BF16)],
        compiler_params=params(),
        cost_estimate=cost(1),
        name="join_pieces",
    )(g03, g12)


def dot_nt(a, b):
    return lax.dot_general(a, b, (((1,), (1,)), ((), ())), preferred_element_type=F32)


def dot_tn(a, b):
    return lax.dot_general(a, b, (((0,), (0,)), ((), ())), preferred_element_type=F32)


def dot_nn(a, b):
    return lax.dot_general(a, b, (((1,), (0,)), ((), ())), preferred_element_type=F32)


def stack_heads(block, heads):
    return jnp.concatenate([block[:, h * HD : (h + 1) * HD] for h in heads], axis=0)


def unstack_heads(parts):
    heads = [part[i : i + SEG] for part in parts for i in range(0, part.shape[0], SEG)]
    return jnp.concatenate(heads, axis=1)


def row_in_segment(shape):
    return lax.broadcasted_iota(jnp.int32, shape, 0) & (SEG - 1)


def group_columns(g):
    wide = pl.ds(pl.multiple_of(g * WIDE, HD), WIDE)
    key = pl.ds(pl.multiple_of(g * HD, HD), HD)
    return wide, key, pl.ds(pl.multiple_of((g + 4) * HD, HD), HD)


CHUNKS = (range(0, 4), range(4, 7))


def backward_kernel(len_ref, q_ref, do_ref, cache_ref, gq_ref, kv_ref):
    third, fourth = len_ref[2], len_ref[3]
    base = cache_ref.shape[0] - 2 * SEG
    offset = 2 * SEG - fourth - third

    @pl.loop(0, 4)
    def _(g):
        wide, key, value = group_columns(g)
        keys, values = cache_ref[:, key], cache_ref[:, value]
        queries = q_ref[:, wide]
        live = lax.broadcasted_iota(jnp.int32, (SEG, WIDE), 0) < third
        douts = jnp.where(live, do_ref[:, wide], jnp.zeros((SEG, WIDE), BF16))
        dk = jnp.zeros((2 * SEG, HD), F32)
        dv = jnp.zeros((2 * SEG, HD), F32)
        grads = []
        for heads in CHUNKS:
            q, dout = stack_heads(queries, heads), stack_heads(douts, heads)
            scores = dot_nt(q, keys)
            along = dot_nt(dout, values)
            shape = (q.shape[0], 2 * SEG)
            ok = lax.broadcasted_iota(jnp.int32, shape, 1) <= offset + row_in_segment(shape)
            tail = jnp.where(ok, scores[:, base:], -1e30)
            scores = jnp.concatenate([scores[:, :base], tail], axis=1)
            top = jnp.max(scores, axis=1, keepdims=True)
            raised = jnp.exp2((scores - top) * EXP_SCALE)
            probs = raised * (1.0 / jnp.sum(raised, axis=1, keepdims=True))
            weighed = probs * along
            delta = jnp.sum(weighed, axis=1, keepdims=True)
            dscore = (weighed - probs * delta).astype(BF16)
            grads.append((dot_nn(dscore, keys) * SCALE).astype(BF16))
            dk = dk + dot_tn(dscore[:, base:], q)
            dv = dv + dot_tn(probs[:, base:].astype(BF16), dout)
        gq_ref[:, wide] = unstack_heads(grads)
        keep = lax.broadcasted_iota(jnp.int32, (SEG, HD), 0) < third
        shift = (2 * SEG - offset) & (2 * SEG - 1)
        dk = pltpu.roll(dk * SCALE, shift, 0)[:SEG]
        dv = pltpu.roll(dv, shift, 0)[:SEG]
        kv_ref[:, key] = jnp.where(keep, dk, 0.0).astype(BF16)
        kv_ref[:, value] = jnp.where(keep, dv, 0.0).astype(BF16)


def backward_groups(lengths, q, dout, cache):
    vmem = pl.BlockSpec(memory_space=pltpu.VMEM)
    return pl.pallas_call(
        backward_kernel,
        out_shape=[
            jax.ShapeDtypeStruct(q.shape, BF16),
            jax.ShapeDtypeStruct((SEG, 8 * HD), BF16),
        ],
        in_specs=[pl.BlockSpec(memory_space=pltpu.SMEM)] + [vmem] * 3,
        out_specs=[vmem] * 2,
        compiler_params=params(),
        cost_estimate=cost(7),
        name="backward_groups",
    )(lengths, q, dout, cache)


def stored_kernel(first, len_ref, q_ref, cache_ref, acc_ref, stat_ref):
    fourth = len_ref[3]
    base = cache_ref.shape[0] - HD

    @pl.loop(0, 2)
    def _(i):
        wide, key, value = group_columns(i + first)
        keys, values = cache_ref[:, key], cache_ref[:, value]
        queries = q_ref[:, wide]
        lane = lax.broadcasted_iota(jnp.int32, (SEG, HD), 1)
        stat = jnp.zeros((SEG, HD), F32)
        mixed = []
        for heads in CHUNKS:
            q = stack_heads(queries, heads)
            scores = dot_nt(q, keys)
            ok = lax.broadcasted_iota(jnp.int32, (q.shape[0], HD), 1) < HD - fourth
            tail = jnp.where(ok, scores[:, base:], -1e30)
            scores = jnp.concatenate([scores[:, :base], tail], axis=1)
            top = jnp.max(scores, axis=1, keepdims=True)
            raised = jnp.exp2((scores - top) * EXP_SCALE)
            total = jnp.sum(raised, axis=1, keepdims=True)
            mixed.append(dot_nn(raised.astype(BF16), values))
            for at, h in enumerate(heads):
                rows = slice(at * SEG, (at + 1) * SEG)
                stat = jnp.where(lane == h, top[rows], stat)
                stat = jnp.where(lane == SEG + h, total[rows], stat)
        wide, key, _ = group_columns(i)
        acc_ref[:, wide] = unstack_heads(mixed)
        stat_ref[:, key] = stat


def stored_groups(lengths, q, cache, first):
    vmem = pl.BlockSpec(memory_space=pltpu.VMEM)
    return pl.pallas_call(
        functools.partial(stored_kernel, first),
        out_shape=[
            jax.ShapeDtypeStruct((SEG, 2 * WIDE), F32),
            jax.ShapeDtypeStruct((SEG, 2 * HD), F32),
        ],
        in_specs=[pl.BlockSpec(memory_space=pltpu.SMEM)] + [vmem] * 2,
        out_specs=[vmem] * 2,
        compiler_params=params(),
        cost_estimate=cost(2.4),
        name="stored_groups",
    )(lengths, q, cache)


def own_kernel(len_ref, q_ref, k0, k1, k3, acc_a, stat_a, acc_b, stat_b, out_ref):
    fourth = len_ref[3]
    own = (k0[...] + k1[0:SEG, :].astype(F32) + k3[...].astype(F32)).astype(BF16)
    shape = (ROWS, SEG)
    at, row = lax.broadcasted_iota(jnp.int32, shape, 1), row_in_segment(shape)
    ok = (at <= row) & (at < fourth)
    heads = range(GROUP)
    for g in range(4):
        acc_ref, stat_ref = ((acc_a, stat_a), (acc_b, stat_b))[g // 2]
        i = g % 2
        q = stack_heads(q_ref[:, g * WIDE : (g + 1) * WIDE], heads)
        acc = stack_heads(acc_ref[:, i * WIDE : (i + 1) * WIDE], heads)
        stat = stat_ref[:, i * HD : (i + 1) * HD]
        top_c = jnp.concatenate([stat[:, h : h + 1] for h in heads], axis=0)
        total_c = jnp.concatenate([stat[:, SEG + h : SEG + h + 1] for h in heads], axis=0)
        scores = jnp.where(ok, dot_nt(q, own[:, g * HD : (g + 1) * HD]), -1e30)
        top = jnp.maximum(top_c, jnp.max(scores, axis=1, keepdims=True))
        keep = jnp.exp2((top_c - top) * EXP_SCALE)
        raised = jnp.exp2((scores - top) * EXP_SCALE)
        total = total_c * keep + jnp.sum(raised, axis=1, keepdims=True)
        values = own[:, (g + 4) * HD : (g + 5) * HD]
        mixed = acc * keep + dot_nn(raised.astype(BF16), values)
        mixed = mixed * (1.0 / total)
        mixed = jnp.where(row_in_segment((ROWS, HD)) < fourth, mixed, 0.0)
        out_ref[:, g * WIDE : (g + 1) * WIDE] = unstack_heads([mixed.astype(BF16)])


def own_groups(lengths, q, parts, held):
    vmem = pl.BlockSpec(memory_space=pltpu.VMEM)
    return pl.pallas_call(
        own_kernel,
        out_shape=jax.ShapeDtypeStruct(q.shape, BF16),
        in_specs=[pl.BlockSpec(memory_space=pltpu.SMEM)] + [vmem] * 8,
        out_specs=vmem,
        compiler_params=params(),
        cost_estimate=cost(2),
        name="own_groups",
    )(lengths, q, *parts, *held)


def own_kv_kernel(r0, r1, r2, r3, a_ref, b_ref, o0, o12, o3, weight_ref, scr):
    _, _, y, c = place()
    for rc, part in enumerate((a_ref, b_ref)):
        for m, r in enumerate((0, 1, 3, 2)):
            for rz in range(2):
                at = (2 * m + rz) * BLK
                scr[rz * 8 + (y ^ r) * 2 + (c ^ rc)] = part[at : at + BLK, :]
    weight = jnp.concatenate([scr[s] for s in range(16)], axis=0)
    weight_ref[...] = weight
    x = jnp.concatenate([r[0:SEG, :] for r in (r0, r1, r2, r3)], axis=0)
    total = dot_nn(x, weight)
    o0[...] = total[0:SEG]
    o12[...] = total[SEG : 3 * SEG].astype(BF16)
    o3[...] = total[3 * SEG :]


def own_kv_parts(pieces, halves):
    vmem = pl.BlockSpec(memory_space=pltpu.VMEM)
    cols = halves[0].shape[1]
    return pl.pallas_call(
        own_kv_kernel,
        out_shape=[
            jax.ShapeDtypeStruct((SEG, cols), F32),
            jax.ShapeDtypeStruct((2 * SEG, cols), BF16),
            jax.ShapeDtypeStruct((SEG, cols), F32),
            jax.ShapeDtypeStruct((2 * PART, cols), BF16),
        ],
        in_specs=[vmem] * 6,
        out_specs=[vmem] * 4,
        scratch_shapes=[pltpu.VMEM((16, BLK, cols), BF16)],
        compiler_params=params(),
        cost_estimate=cost(1.5),
        name="own_kv_parts",
    )(*pieces, *halves)


def token_grads(r0, r1, r2, r3, g0, g1, g32):
    x = jnp.concatenate([r[SEG:, :] for r in (r0, r1, r3, r2)], axis=0)
    grads = jnp.concatenate([g0[...], g1[...], g32[...]], axis=0)
    return dot_tn(x, grads)


def half_rows(total, side):
    _, _, y, c = place()
    blocks = []
    for r in range(4):
        for rz in range(2):
            start = pl.multiple_of(rz * PART + ((y ^ r) * 2 + (c ^ side)) * BLK, 8)
            blocks.append(total[pl.ds(start, BLK), :])
    return blocks


def weight_grad_kernel(r0, r1, r2, r3, g0, g1, g32, away_ref, home_ref, total):
    total[...] = token_grads(r0, r1, r2, r3, g0, g1, g32)
    away_ref[...] = jnp.concatenate(half_rows(total, 1), axis=0).astype(BF16)
    home_ref[...] = jnp.concatenate(half_rows(total, 0), axis=0)


def weight_grad_halves(pieces, grads):
    vmem = pl.BlockSpec(memory_space=pltpu.VMEM)
    cols = grads[0].shape[1]
    return pl.pallas_call(
        weight_grad_kernel,
        out_shape=[
            jax.ShapeDtypeStruct((PART, cols), BF16),
            jax.ShapeDtypeStruct((PART, cols), F32),
        ],
        in_specs=[vmem] * 7,
        out_specs=[vmem] * 2,
        scratch_shapes=[pltpu.VMEM((2 * PART, cols), F32)],
        compiler_params=params(),
        cost_estimate=cost(1.5),
        name="weight_grad_halves",
    )(*pieces, *grads)


def chip_sum_kernel(home_ref, other_ref, s0, s12, s3):
    rows = 2 * BLK
    total = home_ref[...] + other_ref[...].astype(F32)
    s0[...] = total[:rows]
    s12[...] = total[rows : 3 * rows].astype(BF16)
    s3[...] = total[3 * rows :]


def chip_sum(home, other):
    vmem = pl.BlockSpec(memory_space=pltpu.VMEM)
    cols = home.shape[1]
    return pl.pallas_call(
        chip_sum_kernel,
        out_shape=[
            jax.ShapeDtypeStruct((2 * BLK, cols), F32),
            jax.ShapeDtypeStruct((4 * BLK, cols), BF16),
            jax.ShapeDtypeStruct((2 * BLK, cols), F32),
        ],
        in_specs=[vmem] * 2,
        out_specs=[vmem] * 3,
        compiler_params=params(),
        cost_estimate=cost(0.5),
        name="chip_sum",
    )(home, other)


def input_grad_kernel(g0, g1, g32, weight_ref, o0, o1, o32):
    grads = jnp.concatenate([g0[...], g1[...], g32[...]], axis=0)
    total = dot_nt(grads, weight_ref[...]).astype(BF16)
    o0[...] = total[0:SEG]
    o1[...] = total[SEG : 2 * SEG]
    o32[...] = total[2 * SEG :]


def input_grad_pieces(grads, weight):
    vmem = pl.BlockSpec(memory_space=pltpu.VMEM)
    return pl.pallas_call(
        input_grad_kernel,
        out_shape=[
            jax.ShapeDtypeStruct((SEG, 2 * PART), BF16),
            jax.ShapeDtypeStruct((SEG, 2 * PART), BF16),
            jax.ShapeDtypeStruct((2 * SEG, 2 * PART), BF16),
        ],
        in_specs=[vmem] * 4,
        out_specs=[vmem] * 3,
        compiler_params=params(),
        cost_estimate=cost(0.8),
        name="input_grad_pieces",
    )(*grads, weight)


def shards(fwd_x, fwd_q, bwd_x, bwd_q, bwd_dout, cache_kv, kv_weight, seg_lengths):
    shard = kv_weight[0]
    lengths = seg_lengths[0, 0]
    cache = cache_kv[0, 0]
    front_q, back_q, back_dout = fwd_q[0, 0], bwd_q[0, 0], bwd_dout[0, 0]
    together = lax.optimization_barrier
    rows = functools.partial(jnp.concatenate, axis=0)

    across = swap(shard, z=1)
    split = split_inputs(fwd_x[0, 0], bwd_x[0, 0])
    pieces = [split[0]] + [swap(split[r], x=r) for r in (1, 2, 3)]

    pair = rows([shard, across])
    token, pair, pieces[0] = together((lengths, pair, pieces[0]))
    pair_came = swap(pair, y=1)
    grad_query, kv_grad = backward_groups(token, back_q, back_dout, cache)
    pairs = rows([pair, pair_came])
    token, kv_grad, pairs, *pieces = together((lengths, kv_grad, pairs, *pieces))
    kv_came = swap(kv_grad, x=1)
    pairs_came = swap(pairs, y=3)
    held_a = stored_groups(token, front_q, cache, 0)

    kv_pair = rows([kv_grad, kv_came])
    token, kv_pair, *held_a = together((lengths, kv_pair, *held_a))
    grads = (kv_grad, kv_came, swap(kv_pair, x=3))
    held_b = stored_groups(token, front_q, cache, 2)

    half = rows([pairs, pairs_came])
    half, *grads, acc, stat = together((half, *grads, *held_b))
    held = (*held_a, acc, stat)
    other_half = swap(half, c=1)
    away, home = weight_grad_halves(pieces, grads)
    away, other_half, *pieces = together((away, other_half, *pieces))
    other_away = swap(away, c=1)
    own0, own12, own3, weight = own_kv_parts(pieces, (half, other_half))
    own12, weight = together((own12, weight))
    own_came = swap(own12, x=1)
    in0, in1, in32 = input_grad_pieces(grads, weight)
    in_came = swap(in32, x=3)
    other_away, in0 = together((other_away, in0))
    sum0, sum12, sum3 = chip_sum(home, other_away)
    sum_came = swap(sum12, y=1)

    own_came = together((own_came, sum12))[0]
    own_leave = (own3 + own_came[SEG:].astype(F32)).astype(BF16)
    own_last = swap(own_leave, x=3)
    in_came = together((in_came, own_leave))[0]
    leave03 = rows([in0, in_came[:SEG]])
    leave12 = rows([in1, in_came[SEG:]])
    back03 = swap_back_section(leave03)
    back12 = swap_back_section(leave12, x=1)
    token = together((lengths, leave03, leave12))[0]
    fwd_out = own_groups(token, front_q, (own0, own_came, own_last), held)
    next_act = lax.ppermute(fwd_out, "pipe", [(p, p + 1) for p in range(3)])

    sum_came = together((sum_came, fwd_out))[0]
    sum_leave = (sum3 + sum_came[2 * BLK :].astype(F32)).astype(BF16)
    sum_last = swap(sum_leave, y=3)
    total = sum0 + sum_came[: 2 * BLK].astype(F32) + sum_last.astype(F32)
    far_total = total[BLK:].astype(BF16)
    far_came = swap(far_total, z=1)
    back03 = together((back03, far_total))[0]
    prev_grad = join_pieces(back03, back12)
    weight_grad = total[:BLK] + far_came.astype(F32)
    return (next_act[None, None], grad_query[None, None], prev_grad[None, None], weight_grad[None])


def solution(mesh):
    return jax.shard_map(
        shards,
        mesh=mesh,
        in_specs=(
            P("pipe", "dp", None, None),
            P("pipe", "dp", None, None),
            P("pipe", "dp", None, None),
            P("pipe", "dp", None, None),
            P("pipe", "dp", None, None),
            P("pipe", "dp", None, None),
            P("pipe", "dp", None),
            P("pipe", "dp", None),
        ),
        out_specs=(
            P("pipe", "dp", None, None),
            P("pipe", "dp", None, None),
            P("pipe", "dp", None, None),
            P("pipe", "dp", None),
        ),
        check_vma=False,
    )
```

```python
import functools
import math

import jax
import jax.numpy as jnp
from jax import lax
from jax.experimental import pallas as pl
from jax.experimental.pallas import tpu as pltpu
from jax.sharding import PartitionSpec as P

HD = 128
GROUP = 7
SEG = 64
BLK = 56
PART = 8 * BLK
ROWS = GROUP * SEG
WIDE = GROUP * HD
SCALE = 1.0 / math.sqrt(HD)
EXP_SCALE = SCALE * math.log2(math.e)
F32 = jnp.float32
BF16 = jnp.bfloat16
VMEM_LIMIT = 32 * 1024 * 1024
VMEM_MOST = 60 * 1024 * 1024


def params(limit=VMEM_LIMIT):
    return pltpu.CompilerParams(vmem_limit_bytes=limit)


def cost(us):
    return pl.CostEstimate(
        flops=int(us * 0.5e9), bytes_accessed=int(us * 1e6), transcendentals=0
    )


def partner(d, z=0, x=0, y=0, c=0):
    return d ^ (z * 32 + x * 8 + y * 2 + c)


def place():
    d = lax.axis_index("dp")
    return d >> 5, (d >> 3) & 3, (d >> 1) & 3, d & 1


def swap(value, **steps):
    return lax.ppermute(value, "dp", [(d, partner(d, **steps)) for d in range(64)])


def split_kernel(fx_hbm, bx_hbm, o0, o1, o2, o3, fx_ref, bx_ref, scr, sems):
    half = 4 * PART
    copies = []
    for i, (source, held) in enumerate(((fx_hbm, fx_ref), (bx_hbm, bx_ref))):
        for j in range(2):
            cols = pl.ds(j * half, half)
            copy = pltpu.make_async_copy(source.at[:, cols], held.at[:, cols], sems.at[2 * i + j])
            copy.start()
            copies.append(copy)
    for copy in copies:
        copy.wait()
    for s in range(8):
        scr[s, 0:SEG, :] = fx_ref[:, s * PART : (s + 1) * PART]
        scr[s, SEG : 2 * SEG, :] = bx_ref[:, s * PART : (s + 1) * PART]
    z, x, _, _ = place()
    for r, out in enumerate((o0, o1, o2, o3)):
        near = scr[z * 4 + (x ^ r)]
        far = scr[(z ^ 1) * 4 + (x ^ r)]
        out[...] = jnp.concatenate([near, far], axis=1)


def split_inputs(fx, bx):
    vmem = pl.BlockSpec(memory_space=pltpu.VMEM)
    hbm = pl.BlockSpec(memory_space=pltpu.HBM)
    return pl.pallas_call(
        split_kernel,
        out_shape=[jax.ShapeDtypeStruct((2 * SEG, 2 * PART), BF16)] * 4,
        in_specs=[hbm, hbm],
        out_specs=[vmem] * 4,
        scratch_shapes=[
            pltpu.VMEM((SEG, 8 * PART), BF16),
            pltpu.VMEM((SEG, 8 * PART), BF16),
            pltpu.VMEM((8, 2 * SEG, PART), BF16),
            pltpu.SemaphoreType.DMA((4,)),
        ],
        compiler_params=params(VMEM_MOST),
        cost_estimate=cost(1.5),
        name="split_inputs",
    )(fx, bx)


def join_kernel(here, g32, g12, act_ref, out_ref, act_out, scr):
    act_out[...] = act_ref[...]
    z, x, _, _ = place()
    for r, (piece, at) in enumerate(((here, 0), (g12, 0), (g12, SEG), (g32, 0))):
        scr[z * 4 + (x ^ r)] = piece[at : at + SEG, :PART]
        scr[(z ^ 1) * 4 + (x ^ r)] = piece[at : at + SEG, PART:]
    out_ref[...] = jnp.concatenate([scr[s] for s in range(8)], axis=1)


def join_pieces(here, g32, g12, act):
    vmem = pl.BlockSpec(memory_space=pltpu.VMEM)
    return pl.pallas_call(
        join_kernel,
        out_shape=[jax.ShapeDtypeStruct((SEG, 8 * PART), BF16)] * 2,
        in_specs=[vmem] * 4,
        out_specs=[vmem] * 2,
        scratch_shapes=[pltpu.VMEM((8, SEG, PART), BF16)],
        compiler_params=params(),
        cost_estimate=cost(1),
        name="join_pieces",
    )(here, g32, g12, act)


def dot_nt(a, b):
    return lax.dot_general(a, b, (((1,), (1,)), ((), ())), preferred_element_type=F32)


def dot_tn(a, b):
    return lax.dot_general(a, b, (((0,), (0,)), ((), ())), preferred_element_type=F32)


def dot_nn(a, b):
    return lax.dot_general(a, b, (((1,), (0,)), ((), ())), preferred_element_type=F32)


def stack_heads(block, heads):
    return jnp.concatenate([block[:, h * HD : (h + 1) * HD] for h in heads], axis=0)


def unstack_heads(parts):
    heads = [part[i : i + SEG] for part in parts for i in range(0, part.shape[0], SEG)]
    return jnp.concatenate(heads, axis=1)


def row_in_segment(shape):
    return lax.broadcasted_iota(jnp.int32, shape, 0) & (SEG - 1)


def group_columns(g):
    wide = pl.ds(pl.multiple_of(g * WIDE, HD), WIDE)
    key = pl.ds(pl.multiple_of(g * HD, HD), HD)
    return wide, key, pl.ds(pl.multiple_of((g + 4) * HD, HD), HD)


CHUNKS = (range(0, 4), range(4, 7))


def backward_kernel(len_ref, q_ref, do_ref, cache_ref, gq_ref, kv_ref):
    third, fourth = len_ref[2], len_ref[3]
    base = cache_ref.shape[0] - 2 * SEG
    offset = 2 * SEG - fourth - third

    @pl.loop(0, 4)
    def _(g):
        wide, key, value = group_columns(g)
        keys, values = cache_ref[:, key], cache_ref[:, value]
        queries = q_ref[:, wide]
        live = lax.broadcasted_iota(jnp.int32, (SEG, WIDE), 0) < third
        douts = jnp.where(live, do_ref[:, wide], jnp.zeros((SEG, WIDE), BF16))
        dk = jnp.zeros((2 * SEG, HD), F32)
        dv = jnp.zeros((2 * SEG, HD), F32)
        grads = []
        for heads in CHUNKS:
            q, dout = stack_heads(queries, heads), stack_heads(douts, heads)
            scores = dot_nt(q, keys)
            along = dot_nt(dout, values)
            shape = (q.shape[0], 2 * SEG)
            ok = lax.broadcasted_iota(jnp.int32, shape, 1) <= offset + row_in_segment(shape)
            tail = jnp.where(ok, scores[:, base:], -1e30)
            scores = jnp.concatenate([scores[:, :base], tail], axis=1)
            top = jnp.max(scores, axis=1, keepdims=True)
            raised = jnp.exp2((scores - top) * EXP_SCALE)
            probs = raised * (1.0 / jnp.sum(raised, axis=1, keepdims=True))
            weighed = probs * along
            delta = jnp.sum(weighed, axis=1, keepdims=True)
            dscore = (weighed - probs * delta).astype(BF16)
            grads.append((dot_nn(dscore, keys) * SCALE).astype(BF16))
            dk = dk + dot_tn(dscore[:, base:], q)
            dv = dv + dot_tn(probs[:, base:].astype(BF16), dout)
        gq_ref[:, wide] = unstack_heads(grads)
        keep = lax.broadcasted_iota(jnp.int32, (SEG, HD), 0) < third
        shift = (2 * SEG - offset) & (2 * SEG - 1)
        dk = pltpu.roll(dk * SCALE, shift, 0)[:SEG]
        dv = pltpu.roll(dv, shift, 0)[:SEG]
        kv_ref[:, key] = jnp.where(keep, dk, 0.0).astype(BF16)
        kv_ref[:, value] = jnp.where(keep, dv, 0.0).astype(BF16)


def backward_groups(lengths, q, dout, cache):
    vmem = pl.BlockSpec(memory_space=pltpu.VMEM)
    return pl.pallas_call(
        backward_kernel,
        out_shape=[
            jax.ShapeDtypeStruct(q.shape, BF16),
            jax.ShapeDtypeStruct((SEG, 8 * HD), BF16),
        ],
        in_specs=[pl.BlockSpec(memory_space=pltpu.SMEM)] + [vmem] * 3,
        out_specs=[vmem] * 2,
        compiler_params=params(),
        cost_estimate=cost(7),
        name="backward_groups",
    )(lengths, q, dout, cache)


def stored_kernel(first, len_ref, q_ref, cache_ref, acc_ref, stat_ref):
    fourth = len_ref[3]
    base = cache_ref.shape[0] - HD

    @pl.loop(0, 2)
    def _(i):
        wide, key, value = group_columns(i + first)
        keys, values = cache_ref[:, key], cache_ref[:, value]
        queries = q_ref[:, wide]
        lane = lax.broadcasted_iota(jnp.int32, (SEG, HD), 1)
        stat = jnp.zeros((SEG, HD), F32)
        mixed = []
        for heads in CHUNKS:
            q = stack_heads(queries, heads)
            scores = dot_nt(q, keys)
            ok = lax.broadcasted_iota(jnp.int32, (q.shape[0], HD), 1) < HD - fourth
            tail = jnp.where(ok, scores[:, base:], -1e30)
            scores = jnp.concatenate([scores[:, :base], tail], axis=1)
            top = jnp.max(scores, axis=1, keepdims=True)
            raised = jnp.exp2((scores - top) * EXP_SCALE)
            total = jnp.sum(raised, axis=1, keepdims=True)
            mixed.append(dot_nn(raised.astype(BF16), values))
            for at, h in enumerate(heads):
                rows = slice(at * SEG, (at + 1) * SEG)
                stat = jnp.where(lane == h, top[rows], stat)
                stat = jnp.where(lane == SEG + h, total[rows], stat)
        wide, key, _ = group_columns(i)
        acc_ref[:, wide] = unstack_heads(mixed)
        stat_ref[:, key] = stat


def stored_groups(lengths, q, cache, first):
    vmem = pl.BlockSpec(memory_space=pltpu.VMEM)
    return pl.pallas_call(
        functools.partial(stored_kernel, first),
        out_shape=[
            jax.ShapeDtypeStruct((SEG, 2 * WIDE), F32),
            jax.ShapeDtypeStruct((SEG, 2 * HD), F32),
        ],
        in_specs=[pl.BlockSpec(memory_space=pltpu.SMEM)] + [vmem] * 2,
        out_specs=[vmem] * 2,
        compiler_params=params(),
        cost_estimate=cost(2.4),
        name="stored_groups",
    )(lengths, q, cache)


def own_kernel(len_ref, q_ref, k0, k1, k2, k3, acc_a, stat_a, acc_b, stat_b, out_ref):
    fourth = len_ref[3]
    own = k0[...] + k1[...].astype(F32) + k2[...].astype(F32) + k3[...].astype(F32)
    own = own.astype(BF16)
    shape = (ROWS, SEG)
    at, row = lax.broadcasted_iota(jnp.int32, shape, 1), row_in_segment(shape)
    ok = (at <= row) & (at < fourth)
    heads = range(GROUP)
    for g in range(4):
        acc_ref, stat_ref = ((acc_a, stat_a), (acc_b, stat_b))[g // 2]
        i = g % 2
        q = stack_heads(q_ref[:, g * WIDE : (g + 1) * WIDE], heads)
        acc = stack_heads(acc_ref[:, i * WIDE : (i + 1) * WIDE], heads)
        stat = stat_ref[:, i * HD : (i + 1) * HD]
        top_c = jnp.concatenate([stat[:, h : h + 1] for h in heads], axis=0)
        total_c = jnp.concatenate([stat[:, SEG + h : SEG + h + 1] for h in heads], axis=0)
        scores = jnp.where(ok, dot_nt(q, own[:, g * HD : (g + 1) * HD]), -1e30)
        top = jnp.maximum(top_c, jnp.max(scores, axis=1, keepdims=True))
        keep = jnp.exp2((top_c - top) * EXP_SCALE)
        raised = jnp.exp2((scores - top) * EXP_SCALE)
        total = total_c * keep + jnp.sum(raised, axis=1, keepdims=True)
        values = own[:, (g + 4) * HD : (g + 5) * HD]
        mixed = acc * keep + dot_nn(raised.astype(BF16), values)
        mixed = mixed * (1.0 / total)
        mixed = jnp.where(row_in_segment((ROWS, HD)) < fourth, mixed, 0.0)
        out_ref[:, g * WIDE : (g + 1) * WIDE] = unstack_heads([mixed.astype(BF16)])


def own_groups(lengths, q, parts, held):
    vmem = pl.BlockSpec(memory_space=pltpu.VMEM)
    return pl.pallas_call(
        own_kernel,
        out_shape=jax.ShapeDtypeStruct(q.shape, BF16),
        in_specs=[pl.BlockSpec(memory_space=pltpu.SMEM)] + [vmem] * 9,
        out_specs=vmem,
        compiler_params=params(),
        cost_estimate=cost(2),
        name="own_groups",
    )(lengths, q, *parts, *held)


def own_kv_kernel(r0, r1, r2, r3, a_ref, b_ref, o0, o1, o2, o3, weight_ref, scr):
    _, _, y, c = place()
    for rc, part in enumerate((a_ref, b_ref)):
        for m, r in enumerate((0, 1, 3, 2)):
            for rz in range(2):
                at = (2 * m + rz) * BLK
                scr[rz * 8 + (y ^ r) * 2 + (c ^ rc)] = part[at : at + BLK, :]
    weight = jnp.concatenate([scr[s] for s in range(16)], axis=0)
    weight_ref[...] = weight
    x = jnp.concatenate([r[0:SEG, :] for r in (r0, r1, r2, r3)], axis=0)
    total = dot_nn(x, weight)
    for r, out in enumerate((o0, o1, o2, o3)):
        out[...] = total[r * SEG : (r + 1) * SEG].astype(out.dtype)


def own_kv_parts(pieces, halves):
    vmem = pl.BlockSpec(memory_space=pltpu.VMEM)
    cols = halves[0].shape[1]
    return pl.pallas_call(
        own_kv_kernel,
        out_shape=[
            jax.ShapeDtypeStruct((SEG, cols), F32),
            jax.ShapeDtypeStruct((SEG, cols), BF16),
            jax.ShapeDtypeStruct((SEG, cols), BF16),
            jax.ShapeDtypeStruct((SEG, cols), BF16),
            jax.ShapeDtypeStruct((2 * PART, cols), BF16),
        ],
        in_specs=[vmem] * 6,
        out_specs=[vmem] * 5,
        scratch_shapes=[pltpu.VMEM((16, BLK, cols), BF16)],
        compiler_params=params(),
        cost_estimate=cost(1.5),
        name="own_kv_parts",
    )(*pieces, *halves)


def token_grads(r0, r1, r2, r3, g0, g1, g3, g2):
    x = jnp.concatenate([r[SEG:, :] for r in (r0, r1, r3, r2)], axis=0)
    grads = jnp.concatenate([g0[...], g1[...], g3[...], g2[...]], axis=0)
    return dot_tn(x, grads)


def half_rows(total, side):
    _, _, y, c = place()
    blocks = []
    for r in range(4):
        for rz in range(2):
            start = pl.multiple_of(rz * PART + ((y ^ r) * 2 + (c ^ side)) * BLK, 8)
            blocks.append(total[pl.ds(start, BLK), :])
    return blocks


def weight_grad_kernel(r0, r1, r2, r3, g0, g1, g3, g2, away_ref, home_ref, total):
    total[...] = token_grads(r0, r1, r2, r3, g0, g1, g3, g2)
    away_ref[...] = jnp.concatenate(half_rows(total, 1), axis=0).astype(BF16)
    home_ref[...] = jnp.concatenate(half_rows(total, 0), axis=0)


def weight_grad_halves(pieces, grads):
    vmem = pl.BlockSpec(memory_space=pltpu.VMEM)
    cols = grads[0].shape[1]
    return pl.pallas_call(
        weight_grad_kernel,
        out_shape=[
            jax.ShapeDtypeStruct((PART, cols), BF16),
            jax.ShapeDtypeStruct((PART, cols), F32),
        ],
        in_specs=[vmem] * 8,
        out_specs=[vmem] * 2,
        scratch_shapes=[pltpu.VMEM((2 * PART, cols), F32)],
        compiler_params=params(),
        cost_estimate=cost(1.5),
        name="weight_grad_halves",
    )(*pieces, *grads)


def chip_sum_kernel(home_ref, other_ref, s0, s12, s3):
    rows = 2 * BLK
    total = home_ref[...] + other_ref[...].astype(F32)
    s0[...] = total[:rows]
    s12[...] = total[rows : 3 * rows].astype(BF16)
    s3[...] = total[3 * rows :]


def chip_sum(home, other):
    vmem = pl.BlockSpec(memory_space=pltpu.VMEM)
    cols = home.shape[1]
    return pl.pallas_call(
        chip_sum_kernel,
        out_shape=[
            jax.ShapeDtypeStruct((2 * BLK, cols), F32),
            jax.ShapeDtypeStruct((4 * BLK, cols), BF16),
            jax.ShapeDtypeStruct((2 * BLK, cols), F32),
        ],
        in_specs=[vmem] * 2,
        out_specs=[vmem] * 3,
        compiler_params=params(),
        cost_estimate=cost(0.5),
        name="chip_sum",
    )(home, other)


def input_grad_kernel(g0, g1, g3, g2, weight_ref, out_ref):
    grads = jnp.concatenate([g0[...], g1[...], g3[...], g2[...]], axis=0)
    out_ref[...] = dot_nt(grads, weight_ref[...]).astype(BF16)


def input_grad_pieces(grads, weight):
    vmem = pl.BlockSpec(memory_space=pltpu.VMEM)
    return pl.pallas_call(
        input_grad_kernel,
        out_shape=jax.ShapeDtypeStruct((4 * SEG, 2 * PART), BF16),
        in_specs=[vmem] * 5,
        out_specs=vmem,
        compiler_params=params(),
        cost_estimate=cost(0.8),
        name="input_grad_pieces",
    )(*grads, weight)


def shards(fwd_x, fwd_q, bwd_x, bwd_q, bwd_dout, cache_kv, kv_weight, seg_lengths):
    shard = kv_weight[0]
    lengths = seg_lengths[0, 0]
    cache = cache_kv[0, 0]
    front_q, back_q, back_dout = fwd_q[0, 0], bwd_q[0, 0], bwd_dout[0, 0]
    together = lax.optimization_barrier
    rows = functools.partial(jnp.concatenate, axis=0)

    across = swap(shard, z=1)
    split = split_inputs(fwd_x[0, 0], bwd_x[0, 0])
    pieces = [split[0]] + [swap(split[r], x=r) for r in (1, 2, 3)]

    pair = rows([shard, across])
    token, pair, pieces[0] = together((lengths, pair, pieces[0]))
    pair_came = swap(pair, y=1)
    grad_query, kv_grad = backward_groups(token, back_q, back_dout, cache)
    pairs = rows([pair, pair_came])
    token, kv_grad, pairs, *pieces = together((lengths, kv_grad, pairs, *pieces))
    grads = [kv_grad] + [swap(kv_grad, x=r) for r in (1, 3, 2)]
    pairs_came = swap(pairs, y=3)
    held_a = stored_groups(token, front_q, cache, 0)
    token = together((lengths, held_a[1]))[0]
    held_b = stored_groups(token, front_q, cache, 2)

    half = rows([pairs, pairs_came])
    half, *grads, acc, stat = together((half, *grads, *held_b))
    held = (*held_a, acc, stat)
    other_half = swap(half, c=1)
    away, home = weight_grad_halves(pieces, grads)
    other_away = swap(away, c=1)
    away, other_half, *pieces = together((away, other_half, *pieces))
    own0, own1, own2, own3, weight = own_kv_parts(pieces, (half, other_half))
    own_came = [swap(own2, x=2), swap(own1, x=1), swap(own3, x=3)]
    other_away, weight = together((other_away, weight))
    sum0, sum12, sum3 = chip_sum(home, other_away)
    sum_came = swap(sum12, y=1)
    weight = together((weight, sum12))[0]
    leave = input_grad_pieces(grads, weight)
    here = lax.ppermute(leave, "pipe", [(p + 1, p) for p in range(3)])
    own_came = together((*own_came, leave))[:3]
    own2, own1, own3 = own_came
    fwd_out = own_groups(lengths, front_q, (own0, own1, own2, own3), held)
    next_act = lax.ppermute(fwd_out, "pipe", [(p, p + 1) for p in range(3)])
    sum_came = together((sum_came, fwd_out))[0]
    sum_leave = (sum3 + sum_came[2 * BLK :].astype(F32)).astype(BF16)
    sum_last = swap(sum_leave, y=3)
    here = together((here, sum_leave))[0]
    in_came = swap(here[2 * SEG :], x=3)
    total = sum0 + sum_came[: 2 * BLK].astype(F32) + sum_last.astype(F32)
    far_total = total[BLK:].astype(BF16)
    far_came = swap(far_total, z=1)
    in_came = together((in_came, far_total))[0]
    in_last = swap(rows([here[SEG : 2 * SEG], in_came[SEG:]]), x=1)
    prev_grad, next_act = join_pieces(here, in_came, in_last, next_act)
    weight_grad = total[:BLK] + far_came.astype(F32)
    return (next_act[None, None], grad_query[None, None], prev_grad[None, None], weight_grad[None])


def solution(mesh):
    return jax.shard_map(
        shards,
        mesh=mesh,
        in_specs=(
            P("pipe", "dp", None, None),
            P("pipe", "dp", None, None),
            P("pipe", "dp", None, None),
            P("pipe", "dp", None, None),
            P("pipe", "dp", None, None),
            P("pipe", "dp", None, None),
            P("pipe", "dp", None),
            P("pipe", "dp", None),
        ),
        out_specs=(
            P("pipe", "dp", None, None),
            P("pipe", "dp", None, None),
            P("pipe", "dp", None, None),
            P("pipe", "dp", None),
        ),
        check_vma=False,
    )
```

```python
import functools
import math

import jax
import jax.numpy as jnp
from jax import lax
from jax.experimental import pallas as pl
from jax.experimental.pallas import tpu as pltpu
from jax.sharding import PartitionSpec as P

HD = 128
GROUP = 7
SEG = 64
BLK = 56
PART = 8 * BLK
ROWS = GROUP * SEG
WIDE = GROUP * HD
SCALE = 1.0 / math.sqrt(HD)
EXP_SCALE = SCALE * math.log2(math.e)
F32 = jnp.float32
BF16 = jnp.bfloat16
VMEM_LIMIT = 32 * 1024 * 1024
VMEM_MOST = 60 * 1024 * 1024


def params(limit=VMEM_LIMIT):
    return pltpu.CompilerParams(vmem_limit_bytes=limit)


def cost(us):
    return pl.CostEstimate(
        flops=int(us * 0.5e9), bytes_accessed=int(us * 1e6), transcendentals=0
    )


def partner(d, z=0, x=0, y=0, c=0):
    return d ^ (z * 32 + x * 8 + y * 2 + c)


def place():
    d = lax.axis_index("dp")
    return d >> 5, (d >> 3) & 3, (d >> 1) & 3, d & 1


def swap(value, **steps):
    return lax.ppermute(value, "dp", [(d, partner(d, **steps)) for d in range(64)])


def split_kernel(fx_hbm, bx_hbm, o0, o1, o2, o3, fx_ref, bx_ref, scr, sems):
    half = 4 * PART
    copies = []
    for i, (source, held) in enumerate(((fx_hbm, fx_ref), (bx_hbm, bx_ref))):
        for j in range(2):
            cols = pl.ds(j * half, half)
            copy = pltpu.make_async_copy(source.at[:, cols], held.at[:, cols], sems.at[2 * i + j])
            copy.start()
            copies.append(copy)
    for copy in copies:
        copy.wait()
    for s in range(8):
        scr[s, 0:SEG, :] = fx_ref[:, s * PART : (s + 1) * PART]
        scr[s, SEG : 2 * SEG, :] = bx_ref[:, s * PART : (s + 1) * PART]
    z, x, _, _ = place()
    for r, out in enumerate((o0, o1, o2, o3)):
        near = scr[z * 4 + (x ^ r)]
        far = scr[(z ^ 1) * 4 + (x ^ r)]
        out[...] = jnp.concatenate([near, far], axis=1)


def split_inputs(fx, bx):
    vmem = pl.BlockSpec(memory_space=pltpu.VMEM)
    hbm = pl.BlockSpec(memory_space=pltpu.HBM)
    return pl.pallas_call(
        split_kernel,
        out_shape=[jax.ShapeDtypeStruct((2 * SEG, 2 * PART), BF16)] * 4,
        in_specs=[hbm, hbm],
        out_specs=[vmem] * 4,
        scratch_shapes=[
            pltpu.VMEM((SEG, 8 * PART), BF16),
            pltpu.VMEM((SEG, 8 * PART), BF16),
            pltpu.VMEM((8, 2 * SEG, PART), BF16),
            pltpu.SemaphoreType.DMA((4,)),
        ],
        compiler_params=params(VMEM_MOST),
        cost_estimate=cost(1.5),
        name="split_inputs",
    )(fx, bx)


def join_kernel(g0, g1, g2, g3, act_ref, out_ref, act_out, scr):
    act_out[...] = act_ref[...]
    z, x, _, _ = place()
    for r, piece in enumerate((g0, g1, g2, g3)):
        scr[z * 4 + (x ^ r)] = piece[0:SEG, :PART]
        scr[(z ^ 1) * 4 + (x ^ r)] = piece[0:SEG, PART:]
    out_ref[...] = jnp.concatenate([scr[s] for s in range(8)], axis=1)


def join_pieces(g0, g1, g2, g3, act):
    vmem = pl.BlockSpec(memory_space=pltpu.VMEM)
    return pl.pallas_call(
        join_kernel,
        out_shape=[jax.ShapeDtypeStruct((SEG, 8 * PART), BF16)] * 2,
        in_specs=[vmem] * 5,
        out_specs=[vmem] * 2,
        scratch_shapes=[pltpu.VMEM((8, SEG, PART), BF16)],
        compiler_params=params(),
        cost_estimate=cost(1),
        name="join_pieces",
    )(g0, g1, g2, g3, act)


def dot_nt(a, b):
    return lax.dot_general(a, b, (((1,), (1,)), ((), ())), preferred_element_type=F32)


def dot_tn(a, b):
    return lax.dot_general(a, b, (((0,), (0,)), ((), ())), preferred_element_type=F32)


def dot_nn(a, b):
    return lax.dot_general(a, b, (((1,), (0,)), ((), ())), preferred_element_type=F32)


def stack_heads(block, heads):
    return jnp.concatenate([block[:, h * HD : (h + 1) * HD] for h in heads], axis=0)


def unstack_heads(parts):
    heads = [part[i : i + SEG] for part in parts for i in range(0, part.shape[0], SEG)]
    return jnp.concatenate(heads, axis=1)


def row_in_segment(shape):
    return lax.broadcasted_iota(jnp.int32, shape, 0) & (SEG - 1)


def group_columns(g):
    wide = pl.ds(pl.multiple_of(g * WIDE, HD), WIDE)
    key = pl.ds(pl.multiple_of(g * HD, HD), HD)
    return wide, key, pl.ds(pl.multiple_of((g + 4) * HD, HD), HD)


CHUNKS = (range(0, 4), range(4, 7))


def store_group(g, value, held, out_hbm, sems):
    wide = slice(g * WIDE, (g + 1) * WIDE)
    held[:, wide] = value
    copy = pltpu.make_async_copy(held.at[:, wide], out_hbm.at[:, wide], sems.at[g])
    copy.start()
    return copy


def backward_kernel(len_ref, q_ref, do_ref, cache_ref, gq_hbm, kv_ref, held, sems):
    third, fourth = len_ref[2], len_ref[3]
    base = cache_ref.shape[0] - 2 * SEG
    offset = 2 * SEG - fourth - third
    live = lax.broadcasted_iota(jnp.int32, (SEG, WIDE), 0) < third
    keep = lax.broadcasted_iota(jnp.int32, (SEG, HD), 0) < third
    shift = (2 * SEG - offset) & (2 * SEG - 1)
    shape = (ROWS, 2 * SEG)
    ok = lax.broadcasted_iota(jnp.int32, shape, 1) <= offset + row_in_segment(shape)

    def products(g):
        wide = slice(g * WIDE, (g + 1) * WIDE)
        keys = cache_ref[:, g * HD : (g + 1) * HD]
        values = cache_ref[:, (g + 4) * HD : (g + 5) * HD]
        q = stack_heads(q_ref[:, wide], range(GROUP))
        dout = jnp.where(live, do_ref[:, wide], jnp.zeros((SEG, WIDE), BF16))
        dout = stack_heads(dout, range(GROUP))
        return keys, q, dout, dot_nt(q, keys), dot_nt(dout, values)

    copies = []
    ahead = products(0)
    for g in range(4):
        keys, q, dout, scores, along = ahead
        if g < 3:
            ahead = products(g + 1)
        tail = jnp.where(ok, scores[:, base:], -1e30)
        scores = jnp.concatenate([scores[:, :base], tail], axis=1)
        top = jnp.max(scores, axis=1, keepdims=True)
        raised = jnp.exp2((scores - top) * EXP_SCALE)
        probs = raised * (1.0 / jnp.sum(raised, axis=1, keepdims=True))
        weighed = probs * along
        delta = jnp.sum(weighed, axis=1, keepdims=True)
        dscore = (weighed - probs * delta).astype(BF16)
        grads = unstack_heads([(dot_nn(dscore, keys) * SCALE).astype(BF16)])
        copies.append(store_group(g, grads, held, gq_hbm, sems))
        dk = dot_tn(dscore[:, base:], q) * SCALE
        dv = dot_tn(probs[:, base:].astype(BF16), dout)
        dk = pltpu.roll(dk, shift, 0)[:SEG]
        dv = pltpu.roll(dv, shift, 0)[:SEG]
        kv_ref[:, g * HD : (g + 1) * HD] = jnp.where(keep, dk, 0.0).astype(BF16)
        kv_ref[:, (g + 4) * HD : (g + 5) * HD] = jnp.where(keep, dv, 0.0).astype(BF16)
    for copy in copies:
        copy.wait()


def backward_groups(lengths, q, dout, cache):
    vmem = pl.BlockSpec(memory_space=pltpu.VMEM)
    return pl.pallas_call(
        backward_kernel,
        out_shape=[
            jax.ShapeDtypeStruct(q.shape, BF16),
            jax.ShapeDtypeStruct((SEG, 8 * HD), BF16),
        ],
        in_specs=[pl.BlockSpec(memory_space=pltpu.SMEM)] + [vmem] * 3,
        out_specs=[pl.BlockSpec(memory_space=pltpu.HBM), vmem],
        scratch_shapes=[pltpu.VMEM((SEG, 4 * WIDE), BF16), pltpu.SemaphoreType.DMA((4,))],
        compiler_params=params(),
        cost_estimate=cost(7),
        name="backward_groups",
    )(lengths, q, dout, cache)


def stored_kernel(first, len_ref, q_ref, cache_ref, acc_ref, stat_ref):
    fourth = len_ref[3]
    base = cache_ref.shape[0] - HD

    @pl.loop(0, 2)
    def _(i):
        wide, key, value = group_columns(i + first)
        keys, values = cache_ref[:, key], cache_ref[:, value]
        queries = q_ref[:, wide]
        lane = lax.broadcasted_iota(jnp.int32, (SEG, HD), 1)
        stat = jnp.zeros((SEG, HD), F32)
        mixed = []
        for heads in CHUNKS:
            q = stack_heads(queries, heads)
            scores = dot_nt(q, keys)
            ok = lax.broadcasted_iota(jnp.int32, (q.shape[0], HD), 1) < HD - fourth
            tail = jnp.where(ok, scores[:, base:], -1e30)
            scores = jnp.concatenate([scores[:, :base], tail], axis=1)
            top = jnp.max(scores, axis=1, keepdims=True)
            raised = jnp.exp2((scores - top) * EXP_SCALE)
            total = jnp.sum(raised, axis=1, keepdims=True)
            mixed.append(dot_nn(raised.astype(BF16), values))
            for at, h in enumerate(heads):
                rows = slice(at * SEG, (at + 1) * SEG)
                stat = jnp.where(lane == h, top[rows], stat)
                stat = jnp.where(lane == SEG + h, total[rows], stat)
        wide, key, _ = group_columns(i)
        acc_ref[:, wide] = unstack_heads(mixed)
        stat_ref[:, key] = stat


def stored_groups(lengths, q, cache, first):
    vmem = pl.BlockSpec(memory_space=pltpu.VMEM)
    return pl.pallas_call(
        functools.partial(stored_kernel, first),
        out_shape=[
            jax.ShapeDtypeStruct((SEG, 2 * WIDE), F32),
            jax.ShapeDtypeStruct((SEG, 2 * HD), F32),
        ],
        in_specs=[pl.BlockSpec(memory_space=pltpu.SMEM)] + [vmem] * 2,
        out_specs=[vmem] * 2,
        compiler_params=params(),
        cost_estimate=cost(2.4),
        name="stored_groups",
    )(lengths, q, cache)


def own_kernel(len_ref, q_ref, k0, k1, k2, k3, acc_a, stat_a, acc_b, stat_b, out_ref):
    fourth = len_ref[3]
    own = k0[...] + k1[...].astype(F32) + k2[...].astype(F32) + k3[...].astype(F32)
    own = own.astype(BF16)
    shape = (ROWS, SEG)
    at, row = lax.broadcasted_iota(jnp.int32, shape, 1), row_in_segment(shape)
    ok = (at <= row) & (at < fourth)
    heads = range(GROUP)
    for g in range(4):
        acc_ref, stat_ref = ((acc_a, stat_a), (acc_b, stat_b))[g // 2]
        i = g % 2
        q = stack_heads(q_ref[:, g * WIDE : (g + 1) * WIDE], heads)
        acc = stack_heads(acc_ref[:, i * WIDE : (i + 1) * WIDE], heads)
        stat = stat_ref[:, i * HD : (i + 1) * HD]
        top_c = jnp.concatenate([stat[:, h : h + 1] for h in heads], axis=0)
        total_c = jnp.concatenate([stat[:, SEG + h : SEG + h + 1] for h in heads], axis=0)
        scores = jnp.where(ok, dot_nt(q, own[:, g * HD : (g + 1) * HD]), -1e30)
        top = jnp.maximum(top_c, jnp.max(scores, axis=1, keepdims=True))
        keep = jnp.exp2((top_c - top) * EXP_SCALE)
        raised = jnp.exp2((scores - top) * EXP_SCALE)
        total = total_c * keep + jnp.sum(raised, axis=1, keepdims=True)
        values = own[:, (g + 4) * HD : (g + 5) * HD]
        mixed = acc * keep + dot_nn(raised.astype(BF16), values)
        mixed = mixed * (1.0 / total)
        mixed = jnp.where(row_in_segment((ROWS, HD)) < fourth, mixed, 0.0)
        out_ref[:, g * WIDE : (g + 1) * WIDE] = unstack_heads([mixed.astype(BF16)])


def own_groups(lengths, q, parts, held):
    vmem = pl.BlockSpec(memory_space=pltpu.VMEM)
    return pl.pallas_call(
        own_kernel,
        out_shape=jax.ShapeDtypeStruct(q.shape, BF16),
        in_specs=[pl.BlockSpec(memory_space=pltpu.SMEM)] + [vmem] * 9,
        out_specs=vmem,
        compiler_params=params(),
        cost_estimate=cost(2),
        name="own_groups",
    )(lengths, q, *parts, *held)


def own_kv_kernel(r0, r1, r2, r3, a_ref, b_ref, o0, o1, o2, o3, weight_ref, scr):
    _, _, y, c = place()
    for rc, part in enumerate((a_ref, b_ref)):
        for m, r in enumerate((0, 1, 3, 2)):
            for rz in range(2):
                at = (2 * m + rz) * BLK
                scr[rz * 8 + (y ^ r) * 2 + (c ^ rc)] = part[at : at + BLK, :]
    weight = jnp.concatenate([scr[s] for s in range(16)], axis=0)
    weight_ref[...] = weight
    x = jnp.concatenate([r[0:SEG, :] for r in (r0, r1, r2, r3)], axis=0)
    total = dot_nn(x, weight)
    for r, out in enumerate((o0, o1, o2, o3)):
        out[...] = total[r * SEG : (r + 1) * SEG].astype(out.dtype)


def own_kv_parts(pieces, halves):
    vmem = pl.BlockSpec(memory_space=pltpu.VMEM)
    cols = halves[0].shape[1]
    return pl.pallas_call(
        own_kv_kernel,
        out_shape=[
            jax.ShapeDtypeStruct((SEG, cols), F32),
            jax.ShapeDtypeStruct((SEG, cols), BF16),
            jax.ShapeDtypeStruct((SEG, cols), BF16),
            jax.ShapeDtypeStruct((SEG, cols), BF16),
            jax.ShapeDtypeStruct((2 * PART, cols), BF16),
        ],
        in_specs=[vmem] * 6,
        out_specs=[vmem] * 5,
        scratch_shapes=[pltpu.VMEM((16, BLK, cols), BF16)],
        compiler_params=params(),
        cost_estimate=cost(1.5),
        name="own_kv_parts",
    )(*pieces, *halves)


def token_grads(r0, r1, r2, r3, g0, g1, g3, g2):
    x = jnp.concatenate([r[SEG:, :] for r in (r0, r1, r3, r2)], axis=0)
    grads = jnp.concatenate([g0[...], g1[...], g3[...], g2[...]], axis=0)
    return dot_tn(x, grads)


def half_rows(total, side):
    _, _, y, c = place()
    blocks = []
    for r in range(4):
        for rz in range(2):
            start = pl.multiple_of(rz * PART + ((y ^ r) * 2 + (c ^ side)) * BLK, 8)
            blocks.append(total[pl.ds(start, BLK), :])
    return blocks


def weight_grad_kernel(r0, r1, r2, r3, g0, g1, g3, g2, away_ref, home_ref, total):
    total[...] = token_grads(r0, r1, r2, r3, g0, g1, g3, g2)
    away_ref[...] = jnp.concatenate(half_rows(total, 1), axis=0).astype(BF16)
    home_ref[...] = jnp.concatenate(half_rows(total, 0), axis=0)


def weight_grad_halves(pieces, grads):
    vmem = pl.BlockSpec(memory_space=pltpu.VMEM)
    cols = grads[0].shape[1]
    return pl.pallas_call(
        weight_grad_kernel,
        out_shape=[
            jax.ShapeDtypeStruct((PART, cols), BF16),
            jax.ShapeDtypeStruct((PART, cols), F32),
        ],
        in_specs=[vmem] * 8,
        out_specs=[vmem] * 2,
        scratch_shapes=[pltpu.VMEM((2 * PART, cols), F32)],
        compiler_params=params(),
        cost_estimate=cost(1.5),
        name="weight_grad_halves",
    )(*pieces, *grads)


def chip_sum_kernel(home_ref, other_ref, s0, s12, s3):
    rows = 2 * BLK
    total = home_ref[...] + other_ref[...].astype(F32)
    s0[...] = total[:rows]
    s12[...] = total[rows : 3 * rows].astype(BF16)
    s3[...] = total[3 * rows :]


def chip_sum(home, other):
    vmem = pl.BlockSpec(memory_space=pltpu.VMEM)
    cols = home.shape[1]
    return pl.pallas_call(
        chip_sum_kernel,
        out_shape=[
            jax.ShapeDtypeStruct((2 * BLK, cols), F32),
            jax.ShapeDtypeStruct((4 * BLK, cols), BF16),
            jax.ShapeDtypeStruct((2 * BLK, cols), F32),
        ],
        in_specs=[vmem] * 2,
        out_specs=[vmem] * 3,
        compiler_params=params(),
        cost_estimate=cost(0.5),
        name="chip_sum",
    )(home, other)


def input_grad_kernel(g0, g1, g3, g2, weight_ref, out_ref):
    grads = jnp.concatenate([g0[...], g1[...], g3[...], g2[...]], axis=0)
    out_ref[...] = dot_nt(grads, weight_ref[...]).astype(BF16)


def input_grad_pieces(grads, weight):
    vmem = pl.BlockSpec(memory_space=pltpu.VMEM)
    return pl.pallas_call(
        input_grad_kernel,
        out_shape=jax.ShapeDtypeStruct((4 * SEG, 2 * PART), BF16),
        in_specs=[vmem] * 5,
        out_specs=vmem,
        compiler_params=params(),
        cost_estimate=cost(0.8),
        name="input_grad_pieces",
    )(*grads, weight)


def shards(fwd_x, fwd_q, bwd_x, bwd_q, bwd_dout, cache_kv, kv_weight, seg_lengths):
    shard = kv_weight[0]
    lengths = seg_lengths[0, 0]
    cache = cache_kv[0, 0]
    front_q, back_q, back_dout = fwd_q[0, 0], bwd_q[0, 0], bwd_dout[0, 0]
    together = lax.optimization_barrier
    rows = functools.partial(jnp.concatenate, axis=0)

    across = swap(shard, z=1)
    split = split_inputs(fwd_x[0, 0], bwd_x[0, 0])
    pieces = [split[0]] + [swap(split[r], x=r) for r in (1, 2, 3)]

    pair = rows([shard, across])
    token, pair, pieces[0] = together((lengths, pair, pieces[0]))
    pair_came = swap(pair, y=1)
    grad_query, kv_grad = backward_groups(token, back_q, back_dout, cache)
    pairs = rows([pair, pair_came])
    token, kv_grad, pairs, *came = together((lengths, kv_grad, pairs, *(pieces[r] for r in (2, 1, 3))))
    pieces = [pieces[0], came[1], came[0], came[2]]
    far_kv, left_kv, right_kv = [swap(kv_grad, x=r) for r in (2, 3, 1)]
    grads = [kv_grad, right_kv, left_kv, far_kv]
    pairs_came = swap(pairs, y=3)
    held_a = stored_groups(token, front_q, cache, 0)
    far_kv, left_kv, right_kv, acc, stat = together((far_kv, left_kv, right_kv, *held_a))
    grads = [kv_grad, right_kv, left_kv, far_kv]
    away, home = weight_grad_halves(pieces, grads)
    other_away = swap(away, c=1)
    half = rows([pairs, pairs_came])
    token, half, away = together((lengths, half, away))
    other_half = swap(half, c=1)
    held = (acc, stat, *stored_groups(token, front_q, cache, 2))
    other_away, held_last = together((other_away, held[3]))
    held = (*held[:3], held_last)
    sum0, sum12, sum3 = chip_sum(home, other_away)
    sum_came = swap(sum12, y=1)
    other_half, sum12 = together((other_half, sum12))
    own0, own1, own2, own3, weight = own_kv_parts(pieces, (half, other_half))
    own_came = [swap(own2, x=2), swap(own1, x=1), swap(own3, x=3)]
    leave = input_grad_pieces(grads, weight)
    here = lax.ppermute(leave, "pipe", [(p + 1, p) for p in range(3)])
    own_came = together((*own_came, leave))[:3]
    own2, own1, own3 = own_came
    fwd_out = own_groups(lengths, front_q, (own0, own1, own2, own3), held)
    sum_came = together((sum_came, fwd_out))[0]
    sum_leave = (sum3 + sum_came[2 * BLK :].astype(F32)).astype(BF16)
    fwd_out = together((fwd_out, sum_leave))[0]
    next_act = lax.ppermute(fwd_out, "pipe", [(p, p + 1) for p in range(3)])
    sum_last = swap(sum_leave, y=3)
    here = together((here, sum_leave))[0]
    blocks = [here[at * SEG : (at + 1) * SEG] for at in (0, 1, 3, 2)]
    came = [swap(blocks[r], x=r) for r in (2, 1, 3)]
    total = sum0 + sum_came[: 2 * BLK].astype(F32) + sum_last.astype(F32)
    far_total = total[BLK:].astype(BF16)
    far_came = swap(far_total, z=1)
    came = together((*came, far_total))[:3]
    prev_grad, next_act = join_pieces(blocks[0], came[1], came[0], came[2], next_act)
    far_came = together((far_came, prev_grad))[0]
    weight_grad = total[:BLK] + far_came.astype(F32)
    return (next_act[None, None], grad_query[None, None], prev_grad[None, None], weight_grad[None])


def solution(mesh):
    return jax.shard_map(
        shards,
        mesh=mesh,
        in_specs=(
            P("pipe", "dp", None, None),
            P("pipe", "dp", None, None),
            P("pipe", "dp", None, None),
            P("pipe", "dp", None, None),
            P("pipe", "dp", None, None),
            P("pipe", "dp", None, None),
            P("pipe", "dp", None),
            P("pipe", "dp", None),
        ),
        out_specs=(
            P("pipe", "dp", None, None),
            P("pipe", "dp", None, None),
            P("pipe", "dp", None, None),
            P("pipe", "dp", None),
        ),
        check_vma=False,
    )
```

```python
import functools
import math

import jax
import jax.numpy as jnp
from jax import lax
from jax.experimental import pallas as pl
from jax.experimental.pallas import tpu as pltpu
from jax.sharding import PartitionSpec as P

HD = 128
GROUP = 7
SEG = 64
BLK = 56
PART = 8 * BLK
ROWS = GROUP * SEG
WIDE = GROUP * HD
SCALE = 1.0 / math.sqrt(HD)
EXP_SCALE = SCALE * math.log2(math.e)
F32 = jnp.float32
BF16 = jnp.bfloat16
VMEM_LIMIT = 32 * 1024 * 1024
VMEM_MOST = 60 * 1024 * 1024


def params(limit=VMEM_LIMIT):
    return pltpu.CompilerParams(vmem_limit_bytes=limit)


def cost(us):
    return pl.CostEstimate(
        flops=int(us * 0.5e9), bytes_accessed=int(us * 1e6), transcendentals=0
    )


def partner(d, z=0, x=0, y=0, c=0):
    return d ^ (z * 32 + x * 8 + y * 2 + c)


def place():
    d = lax.axis_index("dp")
    return d >> 5, (d >> 3) & 3, (d >> 1) & 3, d & 1


def swap(value, **steps):
    return lax.ppermute(value, "dp", [(d, partner(d, **steps)) for d in range(64)])


def split_kernel(fx_hbm, bx_hbm, o0, o1, o2, o3, fx_ref, bx_ref, scr, sems):
    half = 4 * PART
    copies = []
    for i, (source, held) in enumerate(((fx_hbm, fx_ref), (bx_hbm, bx_ref))):
        for j in range(2):
            cols = pl.ds(j * half, half)
            copy = pltpu.make_async_copy(source.at[:, cols], held.at[:, cols], sems.at[2 * i + j])
            copy.start()
            copies.append(copy)
    for copy in copies:
        copy.wait()
    for s in range(8):
        scr[s, 0:SEG, :] = fx_ref[:, s * PART : (s + 1) * PART]
        scr[s, SEG : 2 * SEG, :] = bx_ref[:, s * PART : (s + 1) * PART]
    z, x, _, _ = place()
    for r, out in enumerate((o0, o1, o2, o3)):
        near = scr[z * 4 + (x ^ r)]
        far = scr[(z ^ 1) * 4 + (x ^ r)]
        out[...] = jnp.concatenate([near, far], axis=1)


def split_inputs(fx, bx):
    vmem = pl.BlockSpec(memory_space=pltpu.VMEM)
    hbm = pl.BlockSpec(memory_space=pltpu.HBM)
    return pl.pallas_call(
        split_kernel,
        out_shape=[jax.ShapeDtypeStruct((2 * SEG, 2 * PART), BF16)] * 4,
        in_specs=[hbm, hbm],
        out_specs=[vmem] * 4,
        scratch_shapes=[
            pltpu.VMEM((SEG, 8 * PART), BF16),
            pltpu.VMEM((SEG, 8 * PART), BF16),
            pltpu.VMEM((8, 2 * SEG, PART), BF16),
            pltpu.SemaphoreType.DMA((4,)),
        ],
        compiler_params=params(VMEM_MOST),
        cost_estimate=cost(1.5),
        name="split_inputs",
    )(fx, bx)


def join_kernel(g0, g1, g2, g3, act_ref, out_ref, act_out, scr):
    act_out[...] = act_ref[...]
    z, x, _, _ = place()
    for r, piece in enumerate((g0, g1, g2, g3)):
        scr[z * 4 + (x ^ r)] = piece[0:SEG, :PART]
        scr[(z ^ 1) * 4 + (x ^ r)] = piece[0:SEG, PART:]
    out_ref[...] = jnp.concatenate([scr[s] for s in range(8)], axis=1)


def join_pieces(g0, g1, g2, g3, act):
    vmem = pl.BlockSpec(memory_space=pltpu.VMEM)
    return pl.pallas_call(
        join_kernel,
        out_shape=[jax.ShapeDtypeStruct((SEG, 8 * PART), BF16)] * 2,
        in_specs=[vmem] * 5,
        out_specs=[vmem] * 2,
        scratch_shapes=[pltpu.VMEM((8, SEG, PART), BF16)],
        compiler_params=params(),
        cost_estimate=cost(1),
        name="join_pieces",
    )(g0, g1, g2, g3, act)


def dot_nt(a, b):
    return lax.dot_general(a, b, (((1,), (1,)), ((), ())), preferred_element_type=F32)


def dot_tn(a, b):
    return lax.dot_general(a, b, (((0,), (0,)), ((), ())), preferred_element_type=F32)


def dot_nn(a, b):
    return lax.dot_general(a, b, (((1,), (0,)), ((), ())), preferred_element_type=F32)


def stack_heads(block, heads):
    return jnp.concatenate([block[:, h * HD : (h + 1) * HD] for h in heads], axis=0)


def unstack_heads(parts):
    heads = [part[i : i + SEG] for part in parts for i in range(0, part.shape[0], SEG)]
    return jnp.concatenate(heads, axis=1)


def row_in_segment(shape):
    return lax.broadcasted_iota(jnp.int32, shape, 0) & (SEG - 1)


def group_columns(g):
    wide = pl.ds(pl.multiple_of(g * WIDE, HD), WIDE)
    key = pl.ds(pl.multiple_of(g * HD, HD), HD)
    return wide, key, pl.ds(pl.multiple_of((g + 4) * HD, HD), HD)


CHUNKS = (range(0, 4), range(4, 7))


def store_group(g, value, held, out_hbm, sems):
    wide = slice(g * WIDE, (g + 1) * WIDE)
    held[:, wide] = value
    copy = pltpu.make_async_copy(held.at[:, wide], out_hbm.at[:, wide], sems.at[g])
    copy.start()
    return copy


def backward_kernel(len_ref, q_ref, do_ref, cache_ref, gq_hbm, kv_ref, held, sems):
    third, fourth = len_ref[2], len_ref[3]
    base = cache_ref.shape[0] - 2 * SEG
    offset = 2 * SEG - fourth - third
    live = lax.broadcasted_iota(jnp.int32, (SEG, WIDE), 0) < third
    keep = lax.broadcasted_iota(jnp.int32, (SEG, HD), 0) < third
    shift = (2 * SEG - offset) & (2 * SEG - 1)
    shape = (ROWS, 2 * SEG)
    ok = lax.broadcasted_iota(jnp.int32, shape, 1) <= offset + row_in_segment(shape)

    def products(g):
        wide = slice(g * WIDE, (g + 1) * WIDE)
        keys = cache_ref[:, g * HD : (g + 1) * HD]
        values = cache_ref[:, (g + 4) * HD : (g + 5) * HD]
        q = stack_heads(q_ref[:, wide], range(GROUP))
        dout = jnp.where(live, do_ref[:, wide], jnp.zeros((SEG, WIDE), BF16))
        dout = stack_heads(dout, range(GROUP))
        return keys, q, dout, dot_nt(q, keys), dot_nt(dout, values)

    copies = []
    ahead = products(0)
    for g in range(4):
        keys, q, dout, scores, along = ahead
        if g < 3:
            ahead = products(g + 1)
        tail = jnp.where(ok, scores[:, base:], -1e30)
        scores = jnp.concatenate([scores[:, :base], tail], axis=1)
        top = jnp.max(scores, axis=1, keepdims=True)
        raised = jnp.exp2((scores - top) * EXP_SCALE)
        probs = raised * (1.0 / jnp.sum(raised, axis=1, keepdims=True))
        weighed = probs * along
        delta = jnp.sum(weighed, axis=1, keepdims=True)
        dscore = (weighed - probs * delta).astype(BF16)
        grads = unstack_heads([(dot_nn(dscore, keys) * SCALE).astype(BF16)])
        copies.append(store_group(g, grads, held, gq_hbm, sems))
        dk = dot_tn(dscore[:, base:], q) * SCALE
        dv = dot_tn(probs[:, base:].astype(BF16), dout)
        dk = pltpu.roll(dk, shift, 0)[:SEG]
        dv = pltpu.roll(dv, shift, 0)[:SEG]
        kv_ref[:, g * HD : (g + 1) * HD] = jnp.where(keep, dk, 0.0).astype(BF16)
        kv_ref[:, (g + 4) * HD : (g + 5) * HD] = jnp.where(keep, dv, 0.0).astype(BF16)
    for copy in copies:
        copy.wait()


def backward_groups(lengths, q, dout, cache):
    vmem = pl.BlockSpec(memory_space=pltpu.VMEM)
    return pl.pallas_call(
        backward_kernel,
        out_shape=[
            jax.ShapeDtypeStruct(q.shape, BF16),
            jax.ShapeDtypeStruct((SEG, 8 * HD), BF16),
        ],
        in_specs=[pl.BlockSpec(memory_space=pltpu.SMEM)] + [vmem] * 3,
        out_specs=[pl.BlockSpec(memory_space=pltpu.HBM), vmem],
        scratch_shapes=[pltpu.VMEM((SEG, 4 * WIDE), BF16), pltpu.SemaphoreType.DMA((4,))],
        compiler_params=params(),
        cost_estimate=cost(7),
        name="backward_groups",
    )(lengths, q, dout, cache)


def stored_kernel(first, len_ref, q_ref, cache_ref, acc_ref, stat_ref):
    fourth = len_ref[3]
    base = cache_ref.shape[0] - HD

    @pl.loop(0, 2)
    def _(i):
        wide, key, value = group_columns(i + first)
        keys, values = cache_ref[:, key], cache_ref[:, value]
        queries = q_ref[:, wide]
        lane = lax.broadcasted_iota(jnp.int32, (SEG, HD), 1)
        stat = jnp.zeros((SEG, HD), F32)
        mixed = []
        for heads in CHUNKS:
            q = stack_heads(queries, heads)
            scores = dot_nt(q, keys)
            ok = lax.broadcasted_iota(jnp.int32, (q.shape[0], HD), 1) < HD - fourth
            tail = jnp.where(ok, scores[:, base:], -1e30)
            scores = jnp.concatenate([scores[:, :base], tail], axis=1)
            top = jnp.max(scores, axis=1, keepdims=True)
            raised = jnp.exp2((scores - top) * EXP_SCALE)
            total = jnp.sum(raised, axis=1, keepdims=True)
            mixed.append(dot_nn(raised.astype(BF16), values))
            for at, h in enumerate(heads):
                rows = slice(at * SEG, (at + 1) * SEG)
                stat = jnp.where(lane == h, top[rows], stat)
                stat = jnp.where(lane == SEG + h, total[rows], stat)
        wide, key, _ = group_columns(i)
        acc_ref[:, wide] = unstack_heads(mixed)
        stat_ref[:, key] = stat


def stored_groups(lengths, q, cache, first):
    vmem = pl.BlockSpec(memory_space=pltpu.VMEM)
    return pl.pallas_call(
        functools.partial(stored_kernel, first),
        out_shape=[
            jax.ShapeDtypeStruct((SEG, 2 * WIDE), F32),
            jax.ShapeDtypeStruct((SEG, 2 * HD), F32),
        ],
        in_specs=[pl.BlockSpec(memory_space=pltpu.SMEM)] + [vmem] * 2,
        out_specs=[vmem] * 2,
        compiler_params=params(),
        cost_estimate=cost(2.4),
        name="stored_groups",
    )(lengths, q, cache)


def own_kernel(len_ref, q_ref, k0, k1, k2, k3, acc_a, stat_a, acc_b, stat_b, out_ref):
    fourth = len_ref[3]
    own = k0[...] + k1[...].astype(F32) + k2[...].astype(F32) + k3[...].astype(F32)
    own = own.astype(BF16)
    shape = (ROWS, SEG)
    at, row = lax.broadcasted_iota(jnp.int32, shape, 1), row_in_segment(shape)
    ok = (at <= row) & (at < fourth)
    heads = range(GROUP)
    for g in range(4):
        acc_ref, stat_ref = ((acc_a, stat_a), (acc_b, stat_b))[g // 2]
        i = g % 2
        q = stack_heads(q_ref[:, g * WIDE : (g + 1) * WIDE], heads)
        acc = stack_heads(acc_ref[:, i * WIDE : (i + 1) * WIDE], heads)
        stat = stat_ref[:, i * HD : (i + 1) * HD]
        top_c = jnp.concatenate([stat[:, h : h + 1] for h in heads], axis=0)
        total_c = jnp.concatenate([stat[:, SEG + h : SEG + h + 1] for h in heads], axis=0)
        scores = jnp.where(ok, dot_nt(q, own[:, g * HD : (g + 1) * HD]), -1e30)
        top = jnp.maximum(top_c, jnp.max(scores, axis=1, keepdims=True))
        keep = jnp.exp2((top_c - top) * EXP_SCALE)
        raised = jnp.exp2((scores - top) * EXP_SCALE)
        total = total_c * keep + jnp.sum(raised, axis=1, keepdims=True)
        values = own[:, (g + 4) * HD : (g + 5) * HD]
        mixed = acc * keep + dot_nn(raised.astype(BF16), values)
        mixed = mixed * (1.0 / total)
        mixed = jnp.where(row_in_segment((ROWS, HD)) < fourth, mixed, 0.0)
        out_ref[:, g * WIDE : (g + 1) * WIDE] = unstack_heads([mixed.astype(BF16)])


def own_groups(lengths, q, parts, held):
    vmem = pl.BlockSpec(memory_space=pltpu.VMEM)
    return pl.pallas_call(
        own_kernel,
        out_shape=jax.ShapeDtypeStruct(q.shape, BF16),
        in_specs=[pl.BlockSpec(memory_space=pltpu.SMEM)] + [vmem] * 9,
        out_specs=vmem,
        compiler_params=params(),
        cost_estimate=cost(2),
        name="own_groups",
    )(lengths, q, *parts, *held)


def own_kv_kernel(r0, r1, r2, r3, a_ref, b_ref, o0, o1, o2, o3, weight_ref, scr):
    _, _, y, c = place()
    for rc, part in enumerate((a_ref, b_ref)):
        for m, r in enumerate((0, 1, 3, 2)):
            for rz in range(2):
                at = (2 * m + rz) * BLK
                scr[rz * 8 + (y ^ r) * 2 + (c ^ rc)] = part[at : at + BLK, :]
    weight = jnp.concatenate([scr[s] for s in range(16)], axis=0)
    weight_ref[...] = weight
    x = jnp.concatenate([r[0:SEG, :] for r in (r0, r1, r2, r3)], axis=0)
    total = dot_nn(x, weight)
    for r, out in enumerate((o0, o1, o2, o3)):
        out[...] = total[r * SEG : (r + 1) * SEG].astype(out.dtype)


def own_kv_parts(pieces, halves):
    vmem = pl.BlockSpec(memory_space=pltpu.VMEM)
    cols = halves[0].shape[1]
    return pl.pallas_call(
        own_kv_kernel,
        out_shape=[
            jax.ShapeDtypeStruct((SEG, cols), F32),
            jax.ShapeDtypeStruct((SEG, cols), BF16),
            jax.ShapeDtypeStruct((SEG, cols), BF16),
            jax.ShapeDtypeStruct((SEG, cols), BF16),
            jax.ShapeDtypeStruct((2 * PART, cols), BF16),
        ],
        in_specs=[vmem] * 6,
        out_specs=[vmem] * 5,
        scratch_shapes=[pltpu.VMEM((16, BLK, cols), BF16)],
        compiler_params=params(),
        cost_estimate=cost(1.5),
        name="own_kv_parts",
    )(*pieces, *halves)


def token_grads(r0, r1, r2, r3, g0, g1, g3, g2):
    x = jnp.concatenate([r[SEG:, :] for r in (r0, r1, r3, r2)], axis=0)
    grads = jnp.concatenate([g0[...], g1[...], g3[...], g2[...]], axis=0)
    return dot_tn(x, grads)


def half_rows(total, side):
    _, _, y, c = place()
    blocks = []
    for r in range(4):
        for rz in range(2):
            start = pl.multiple_of(rz * PART + ((y ^ r) * 2 + (c ^ side)) * BLK, 8)
            blocks.append(total[pl.ds(start, BLK), :])
    return blocks


def weight_grad_kernel(r0, r1, r2, r3, g0, g1, g3, g2, away_ref, home_ref, total):
    total[...] = token_grads(r0, r1, r2, r3, g0, g1, g3, g2)
    away_ref[...] = jnp.concatenate(half_rows(total, 1), axis=0).astype(BF16)
    home_ref[...] = jnp.concatenate(half_rows(total, 0), axis=0)


def weight_grad_halves(pieces, grads):
    vmem = pl.BlockSpec(memory_space=pltpu.VMEM)
    cols = grads[0].shape[1]
    return pl.pallas_call(
        weight_grad_kernel,
        out_shape=[
            jax.ShapeDtypeStruct((PART, cols), BF16),
            jax.ShapeDtypeStruct((PART, cols), F32),
        ],
        in_specs=[vmem] * 8,
        out_specs=[vmem] * 2,
        scratch_shapes=[pltpu.VMEM((2 * PART, cols), F32)],
        compiler_params=params(),
        cost_estimate=cost(1.5),
        name="weight_grad_halves",
    )(*pieces, *grads)


def chip_sum_kernel(home_ref, other_ref, s0, s12, s3):
    rows = 2 * BLK
    total = home_ref[...] + other_ref[...].astype(F32)
    s0[...] = total[:rows]
    s12[...] = total[rows : 3 * rows].astype(BF16)
    s3[...] = total[3 * rows :]


def chip_sum(home, other):
    vmem = pl.BlockSpec(memory_space=pltpu.VMEM)
    cols = home.shape[1]
    return pl.pallas_call(
        chip_sum_kernel,
        out_shape=[
            jax.ShapeDtypeStruct((2 * BLK, cols), F32),
            jax.ShapeDtypeStruct((4 * BLK, cols), BF16),
            jax.ShapeDtypeStruct((2 * BLK, cols), F32),
        ],
        in_specs=[vmem] * 2,
        out_specs=[vmem] * 3,
        compiler_params=params(),
        cost_estimate=cost(0.5),
        name="chip_sum",
    )(home, other)


def input_grad_kernel(g0, g1, g3, g2, weight_ref, out_ref):
    grads = jnp.concatenate([g0[...], g1[...], g3[...], g2[...]], axis=0)
    out_ref[...] = dot_nt(grads, weight_ref[...]).astype(BF16)


def input_grad_pieces(grads, weight):
    vmem = pl.BlockSpec(memory_space=pltpu.VMEM)
    return pl.pallas_call(
        input_grad_kernel,
        out_shape=jax.ShapeDtypeStruct((4 * SEG, 2 * PART), BF16),
        in_specs=[vmem] * 5,
        out_specs=vmem,
        compiler_params=params(),
        cost_estimate=cost(0.8),
        name="input_grad_pieces",
    )(*grads, weight)


def shards(fwd_x, fwd_q, bwd_x, bwd_q, bwd_dout, cache_kv, kv_weight, seg_lengths):
    shard = kv_weight[0]
    lengths = seg_lengths[0, 0]
    cache = cache_kv[0, 0]
    front_q, back_q, back_dout = fwd_q[0, 0], bwd_q[0, 0], bwd_dout[0, 0]
    together = lax.optimization_barrier
    rows = functools.partial(jnp.concatenate, axis=0)

    across = swap(shard, z=1)
    split = split_inputs(fwd_x[0, 0], bwd_x[0, 0])
    pieces = [split[0]] + [swap(split[r], x=r) for r in (1, 2, 3)]

    pair = rows([shard, across])
    token, pair, pieces[0] = together((lengths, pair, pieces[0]))
    pair_came = swap(pair, y=1)
    grad_query, kv_grad = backward_groups(token, back_q, back_dout, cache)
    pairs = rows([pair, pair_came])
    token, kv_grad, pairs, *came = together((lengths, kv_grad, pairs, *(pieces[r] for r in (2, 1, 3))))
    pieces = [pieces[0], came[1], came[0], came[2]]
    far_kv, left_kv, right_kv = [swap(kv_grad, x=r) for r in (2, 3, 1)]
    grads = [kv_grad, right_kv, left_kv, far_kv]
    pairs_came = swap(pairs, y=3)
    held_a = stored_groups(token, front_q, cache, 0)
    far_kv, left_kv, right_kv, acc, stat = together((far_kv, left_kv, right_kv, *held_a))
    grads = [kv_grad, right_kv, left_kv, far_kv]
    away, home = weight_grad_halves(pieces, grads)
    other_away = swap(away, c=1)
    half = rows([pairs, pairs_came])
    half, away = together((half, away))
    other_half = swap(half, c=1)
    sum0, sum12, sum3 = chip_sum(home, other_away)
    sum_came = swap(sum12, y=1)
    other_half, sum12 = together((other_half, sum12))
    own0, own1, own2, own3, weight = own_kv_parts(pieces, (half, other_half))
    own_came = [swap(own2, x=2), swap(own1, x=1), swap(own3, x=3)]
    leave = input_grad_pieces(grads, weight)
    here = lax.ppermute(leave, "pipe", [(p + 1, p) for p in range(3)])
    token = together((lengths, leave))[0]
    held_b = stored_groups(token, front_q, cache, 2)
    own_came = together((*own_came, held_b[1]))[:3]
    held = (acc, stat, *held_b)
    own2, own1, own3 = own_came
    fwd_out = own_groups(lengths, front_q, (own0, own1, own2, own3), held)
    sum_came = together((sum_came, fwd_out))[0]
    sum_leave = (sum3 + sum_came[2 * BLK :].astype(F32)).astype(BF16)
    fwd_out = together((fwd_out, sum_leave))[0]
    next_act = lax.ppermute(fwd_out, "pipe", [(p, p + 1) for p in range(3)])
    sum_last = swap(sum_leave, y=3)
    here = together((here, sum_leave))[0]
    blocks = [here[at * SEG : (at + 1) * SEG] for at in (0, 1, 3, 2)]
    came = [swap(blocks[r], x=r) for r in (2, 1, 3)]
    total = sum0 + sum_came[: 2 * BLK].astype(F32) + sum_last.astype(F32)
    far_total = total[BLK:].astype(BF16)
    far_came = swap(far_total, z=1)
    came = together((*came, far_total))[:3]
    prev_grad, next_act = join_pieces(blocks[0], came[1], came[0], came[2], next_act)
    far_came = together((far_came, prev_grad))[0]
    weight_grad = total[:BLK] + far_came.astype(F32)
    return (next_act[None, None], grad_query[None, None], prev_grad[None, None], weight_grad[None])


def solution(mesh):
    return jax.shard_map(
        shards,
        mesh=mesh,
        in_specs=(
            P("pipe", "dp", None, None),
            P("pipe", "dp", None, None),
            P("pipe", "dp", None, None),
            P("pipe", "dp", None, None),
            P("pipe", "dp", None, None),
            P("pipe", "dp", None, None),
            P("pipe", "dp", None),
            P("pipe", "dp", None),
        ),
        out_specs=(
            P("pipe", "dp", None, None),
            P("pipe", "dp", None, None),
            P("pipe", "dp", None, None),
            P("pipe", "dp", None),
        ),
        check_vma=False,
    )
```

```python
import functools
import math

import jax
import jax.numpy as jnp
from jax import lax
from jax.experimental import pallas as pl
from jax.experimental.pallas import tpu as pltpu
from jax.sharding import PartitionSpec as P

HD = 128
GROUP = 7
SEG = 64
BLK = 56
PART = 8 * BLK
ROWS = GROUP * SEG
WIDE = GROUP * HD
SCALE = 1.0 / math.sqrt(HD)
EXP_SCALE = SCALE * math.log2(math.e)
F32 = jnp.float32
BF16 = jnp.bfloat16
VMEM_LIMIT = 32 * 1024 * 1024
VMEM_MOST = 60 * 1024 * 1024


def params(limit=VMEM_LIMIT):
    return pltpu.CompilerParams(vmem_limit_bytes=limit)


def cost(us):
    return pl.CostEstimate(
        flops=int(us * 0.5e9), bytes_accessed=int(us * 1e6), transcendentals=0
    )


def partner(d, z=0, x=0, y=0, c=0):
    return d ^ (z * 32 + x * 8 + y * 2 + c)


def place():
    d = lax.axis_index("dp")
    return d >> 5, (d >> 3) & 3, (d >> 1) & 3, d & 1


def swap(value, **steps):
    return lax.ppermute(value, "dp", [(d, partner(d, **steps)) for d in range(64)])


def split_kernel(fx_hbm, bx_hbm, o0, o1, o2, o3, fx_ref, bx_ref, scr, sems):
    half = 4 * PART
    copies = []
    for i, (source, held) in enumerate(((fx_hbm, fx_ref), (bx_hbm, bx_ref))):
        for j in range(2):
            cols = pl.ds(j * half, half)
            copy = pltpu.make_async_copy(source.at[:, cols], held.at[:, cols], sems.at[2 * i + j])
            copy.start()
            copies.append(copy)
    for copy in copies:
        copy.wait()
    for s in range(8):
        scr[s, 0:SEG, :] = fx_ref[:, s * PART : (s + 1) * PART]
        scr[s, SEG : 2 * SEG, :] = bx_ref[:, s * PART : (s + 1) * PART]
    z, x, _, _ = place()
    for r, out in enumerate((o0, o1, o2, o3)):
        near = scr[z * 4 + (x ^ r)]
        far = scr[(z ^ 1) * 4 + (x ^ r)]
        out[...] = jnp.concatenate([near, far], axis=1)


def split_inputs(fx, bx):
    vmem = pl.BlockSpec(memory_space=pltpu.VMEM)
    hbm = pl.BlockSpec(memory_space=pltpu.HBM)
    return pl.pallas_call(
        split_kernel,
        out_shape=[jax.ShapeDtypeStruct((2 * SEG, 2 * PART), BF16)] * 4,
        in_specs=[hbm, hbm],
        out_specs=[vmem] * 4,
        scratch_shapes=[
            pltpu.VMEM((SEG, 8 * PART), BF16),
            pltpu.VMEM((SEG, 8 * PART), BF16),
            pltpu.VMEM((8, 2 * SEG, PART), BF16),
            pltpu.SemaphoreType.DMA((4,)),
        ],
        compiler_params=params(VMEM_MOST),
        cost_estimate=cost(1.5),
        name="split_inputs",
    )(fx, bx)


def join_kernel(g0, g1, g2, g3, act_ref, out_ref, act_out, scr):
    act_out[...] = act_ref[...]
    z, x, _, _ = place()
    for r, piece in enumerate((g0, g1, g2, g3)):
        scr[z * 4 + (x ^ r)] = piece[0:SEG, :PART]
        scr[(z ^ 1) * 4 + (x ^ r)] = piece[0:SEG, PART:]
    out_ref[...] = jnp.concatenate([scr[s] for s in range(8)], axis=1)


def join_pieces(g0, g1, g2, g3, act):
    vmem = pl.BlockSpec(memory_space=pltpu.VMEM)
    return pl.pallas_call(
        join_kernel,
        out_shape=[jax.ShapeDtypeStruct((SEG, 8 * PART), BF16)] * 2,
        in_specs=[vmem] * 5,
        out_specs=[vmem] * 2,
        scratch_shapes=[pltpu.VMEM((8, SEG, PART), BF16)],
        compiler_params=params(),
        cost_estimate=cost(1),
        name="join_pieces",
    )(g0, g1, g2, g3, act)


def dot_nt(a, b):
    return lax.dot_general(a, b, (((1,), (1,)), ((), ())), preferred_element_type=F32)


def dot_tn(a, b):
    return lax.dot_general(a, b, (((0,), (0,)), ((), ())), preferred_element_type=F32)


def dot_nn(a, b):
    return lax.dot_general(a, b, (((1,), (0,)), ((), ())), preferred_element_type=F32)


def stack_heads(block, heads):
    return jnp.concatenate([block[:, h * HD : (h + 1) * HD] for h in heads], axis=0)


def unstack_heads(parts):
    heads = [part[i : i + SEG] for part in parts for i in range(0, part.shape[0], SEG)]
    return jnp.concatenate(heads, axis=1)


def row_in_segment(shape):
    return lax.broadcasted_iota(jnp.int32, shape, 0) & (SEG - 1)


def group_columns(g):
    wide = pl.ds(pl.multiple_of(g * WIDE, HD), WIDE)
    key = pl.ds(pl.multiple_of(g * HD, HD), HD)
    return wide, key, pl.ds(pl.multiple_of((g + 4) * HD, HD), HD)


CHUNKS = (range(0, 4), range(4, 7))


def store_group(g, value, held, out_hbm, sems):
    wide = slice(g * WIDE, (g + 1) * WIDE)
    held[:, wide] = value
    copy = pltpu.make_async_copy(held.at[:, wide], out_hbm.at[:, wide], sems.at[g])
    copy.start()
    return copy


def backward_kernel(len_ref, q_ref, do_ref, cache_ref, gq_hbm, kv_ref, held, sems):
    third, fourth = len_ref[2], len_ref[3]
    base = cache_ref.shape[0] - 2 * SEG
    offset = 2 * SEG - fourth - third
    live = lax.broadcasted_iota(jnp.int32, (SEG, WIDE), 0) < third
    keep = lax.broadcasted_iota(jnp.int32, (SEG, HD), 0) < third
    shift = (2 * SEG - offset) & (2 * SEG - 1)
    shape = (ROWS, 2 * SEG)
    ok = lax.broadcasted_iota(jnp.int32, shape, 1) <= offset + row_in_segment(shape)

    def products(g):
        wide = slice(g * WIDE, (g + 1) * WIDE)
        keys = cache_ref[:, g * HD : (g + 1) * HD]
        values = cache_ref[:, (g + 4) * HD : (g + 5) * HD]
        q = stack_heads(q_ref[:, wide], range(GROUP))
        dout = jnp.where(live, do_ref[:, wide], jnp.zeros((SEG, WIDE), BF16))
        dout = stack_heads(dout, range(GROUP))
        return keys, q, dout, dot_nt(q, keys), dot_nt(dout, values)

    copies = []
    ahead = products(0)
    for g in range(4):
        keys, q, dout, scores, along = ahead
        if g < 3:
            ahead = products(g + 1)
        tail = jnp.where(ok, scores[:, base:], -1e30)
        scores = jnp.concatenate([scores[:, :base], tail], axis=1)
        top = jnp.max(scores, axis=1, keepdims=True)
        raised = jnp.exp2((scores - top) * EXP_SCALE)
        probs = raised * (1.0 / jnp.sum(raised, axis=1, keepdims=True))
        weighed = probs * along
        delta = jnp.sum(weighed, axis=1, keepdims=True)
        dscore = (weighed - probs * delta).astype(BF16)
        grads = unstack_heads([(dot_nn(dscore, keys) * SCALE).astype(BF16)])
        copies.append(store_group(g, grads, held, gq_hbm, sems))
        dk = dot_tn(dscore[:, base:], q) * SCALE
        dv = dot_tn(probs[:, base:].astype(BF16), dout)
        dk = pltpu.roll(dk, shift, 0)[:SEG]
        dv = pltpu.roll(dv, shift, 0)[:SEG]
        kv_ref[:, g * HD : (g + 1) * HD] = jnp.where(keep, dk, 0.0).astype(BF16)
        kv_ref[:, (g + 4) * HD : (g + 5) * HD] = jnp.where(keep, dv, 0.0).astype(BF16)
    for copy in copies:
        copy.wait()


def backward_groups(lengths, q, dout, cache):
    vmem = pl.BlockSpec(memory_space=pltpu.VMEM)
    return pl.pallas_call(
        backward_kernel,
        out_shape=[
            jax.ShapeDtypeStruct(q.shape, BF16),
            jax.ShapeDtypeStruct((SEG, 8 * HD), BF16),
        ],
        in_specs=[pl.BlockSpec(memory_space=pltpu.SMEM)] + [vmem] * 3,
        out_specs=[pl.BlockSpec(memory_space=pltpu.HBM), vmem],
        scratch_shapes=[pltpu.VMEM((SEG, 4 * WIDE), BF16), pltpu.SemaphoreType.DMA((4,))],
        compiler_params=params(),
        cost_estimate=cost(7),
        name="backward_groups",
    )(lengths, q, dout, cache)


def stored_kernel(first, len_ref, q_ref, cache_ref, acc_ref, stat_ref):
    fourth = len_ref[3]
    base = cache_ref.shape[0] - HD

    @pl.loop(0, 2)
    def _(i):
        wide, key, value = group_columns(i + first)
        keys, values = cache_ref[:, key], cache_ref[:, value]
        queries = q_ref[:, wide]
        lane = lax.broadcasted_iota(jnp.int32, (SEG, HD), 1)
        stat = jnp.zeros((SEG, HD), F32)
        mixed = []
        for heads in CHUNKS:
            q = stack_heads(queries, heads)
            scores = dot_nt(q, keys)
            ok = lax.broadcasted_iota(jnp.int32, (q.shape[0], HD), 1) < HD - fourth
            tail = jnp.where(ok, scores[:, base:], -1e30)
            scores = jnp.concatenate([scores[:, :base], tail], axis=1)
            top = jnp.max(scores, axis=1, keepdims=True)
            raised = jnp.exp2((scores - top) * EXP_SCALE)
            total = jnp.sum(raised, axis=1, keepdims=True)
            mixed.append(dot_nn(raised.astype(BF16), values))
            for at, h in enumerate(heads):
                rows = slice(at * SEG, (at + 1) * SEG)
                stat = jnp.where(lane == h, top[rows], stat)
                stat = jnp.where(lane == SEG + h, total[rows], stat)
        wide, key, _ = group_columns(i)
        acc_ref[:, wide] = unstack_heads(mixed)
        stat_ref[:, key] = stat


def stored_groups(lengths, q, cache, first):
    vmem = pl.BlockSpec(memory_space=pltpu.VMEM)
    return pl.pallas_call(
        functools.partial(stored_kernel, first),
        out_shape=[
            jax.ShapeDtypeStruct((SEG, 2 * WIDE), F32),
            jax.ShapeDtypeStruct((SEG, 2 * HD), F32),
        ],
        in_specs=[pl.BlockSpec(memory_space=pltpu.SMEM)] + [vmem] * 2,
        out_specs=[vmem] * 2,
        compiler_params=params(),
        cost_estimate=cost(2.4),
        name="stored_groups",
    )(lengths, q, cache)


def own_kernel(len_ref, q_ref, k0, k1, k2, k3, acc_a, stat_a, acc_b, stat_b, out_ref):
    fourth = len_ref[3]
    own = k0[...] + k1[...].astype(F32) + k2[...].astype(F32) + k3[...].astype(F32)
    own = own.astype(BF16)
    shape = (ROWS, SEG)
    at, row = lax.broadcasted_iota(jnp.int32, shape, 1), row_in_segment(shape)
    ok = (at <= row) & (at < fourth)
    heads = range(GROUP)
    for g in range(4):
        acc_ref, stat_ref = ((acc_a, stat_a), (acc_b, stat_b))[g // 2]
        i = g % 2
        q = stack_heads(q_ref[:, g * WIDE : (g + 1) * WIDE], heads)
        acc = stack_heads(acc_ref[:, i * WIDE : (i + 1) * WIDE], heads)
        stat = stat_ref[:, i * HD : (i + 1) * HD]
        top_c = jnp.concatenate([stat[:, h : h + 1] for h in heads], axis=0)
        total_c = jnp.concatenate([stat[:, SEG + h : SEG + h + 1] for h in heads], axis=0)
        scores = jnp.where(ok, dot_nt(q, own[:, g * HD : (g + 1) * HD]), -1e30)
        top = jnp.maximum(top_c, jnp.max(scores, axis=1, keepdims=True))
        keep = jnp.exp2((top_c - top) * EXP_SCALE)
        raised = jnp.exp2((scores - top) * EXP_SCALE)
        total = total_c * keep + jnp.sum(raised, axis=1, keepdims=True)
        values = own[:, (g + 4) * HD : (g + 5) * HD]
        mixed = acc * keep + dot_nn(raised.astype(BF16), values)
        mixed = mixed * (1.0 / total)
        mixed = jnp.where(row_in_segment((ROWS, HD)) < fourth, mixed, 0.0)
        out_ref[:, g * WIDE : (g + 1) * WIDE] = unstack_heads([mixed.astype(BF16)])


def own_groups(lengths, q, parts, held):
    vmem = pl.BlockSpec(memory_space=pltpu.VMEM)
    return pl.pallas_call(
        own_kernel,
        out_shape=jax.ShapeDtypeStruct(q.shape, BF16),
        in_specs=[pl.BlockSpec(memory_space=pltpu.SMEM)] + [vmem] * 9,
        out_specs=vmem,
        compiler_params=params(),
        cost_estimate=cost(2),
        name="own_groups",
    )(lengths, q, *parts, *held)


def own_kv_kernel(r0, r1, r2, r3, a_ref, b_ref, o0, o1, o2, o3, weight_ref, scr):
    _, _, y, c = place()
    for rc, part in enumerate((a_ref, b_ref)):
        for m, r in enumerate((0, 1, 3, 2)):
            for rz in range(2):
                at = (2 * m + rz) * BLK
                scr[rz * 8 + (y ^ r) * 2 + (c ^ rc)] = part[at : at + BLK, :]
    weight = jnp.concatenate([scr[s] for s in range(16)], axis=0)
    weight_ref[...] = weight
    x = jnp.concatenate([r[0:SEG, :] for r in (r0, r1, r2, r3)], axis=0)
    total = dot_nn(x, weight)
    for r, out in enumerate((o0, o1, o2, o3)):
        out[...] = total[r * SEG : (r + 1) * SEG].astype(out.dtype)


def own_kv_parts(pieces, halves):
    vmem = pl.BlockSpec(memory_space=pltpu.VMEM)
    cols = halves[0].shape[1]
    return pl.pallas_call(
        own_kv_kernel,
        out_shape=[
            jax.ShapeDtypeStruct((SEG, cols), F32),
            jax.ShapeDtypeStruct((SEG, cols), BF16),
            jax.ShapeDtypeStruct((SEG, cols), BF16),
            jax.ShapeDtypeStruct((SEG, cols), BF16),
            jax.ShapeDtypeStruct((2 * PART, cols), BF16),
        ],
        in_specs=[vmem] * 6,
        out_specs=[vmem] * 5,
        scratch_shapes=[pltpu.VMEM((16, BLK, cols), BF16)],
        compiler_params=params(),
        cost_estimate=cost(1.5),
        name="own_kv_parts",
    )(*pieces, *halves)


def token_grads(r0, r1, r2, r3, g0, g1, g3, g2):
    x = jnp.concatenate([r[SEG:, :] for r in (r0, r1, r3, r2)], axis=0)
    grads = jnp.concatenate([g0[...], g1[...], g3[...], g2[...]], axis=0)
    return dot_tn(x, grads)


def half_rows(total, side):
    _, _, y, c = place()
    blocks = []
    for r in range(4):
        for rz in range(2):
            start = pl.multiple_of(rz * PART + ((y ^ r) * 2 + (c ^ side)) * BLK, 8)
            blocks.append(total[pl.ds(start, BLK), :])
    return blocks


def weight_grad_kernel(r0, r1, r2, r3, g0, g1, g3, g2, away_ref, home_ref, total):
    total[...] = token_grads(r0, r1, r2, r3, g0, g1, g3, g2)
    away_ref[...] = jnp.concatenate(half_rows(total, 1), axis=0).astype(BF16)
    home_ref[...] = jnp.concatenate(half_rows(total, 0), axis=0)


def weight_grad_halves(pieces, grads):
    vmem = pl.BlockSpec(memory_space=pltpu.VMEM)
    cols = grads[0].shape[1]
    return pl.pallas_call(
        weight_grad_kernel,
        out_shape=[
            jax.ShapeDtypeStruct((PART, cols), BF16),
            jax.ShapeDtypeStruct((PART, cols), F32),
        ],
        in_specs=[vmem] * 8,
        out_specs=[vmem] * 2,
        scratch_shapes=[pltpu.VMEM((2 * PART, cols), F32)],
        compiler_params=params(),
        cost_estimate=cost(1.5),
        name="weight_grad_halves",
    )(*pieces, *grads)


def chip_sum_kernel(home_ref, other_ref, s0, s12, s3):
    rows = 2 * BLK
    total = home_ref[...] + other_ref[...].astype(F32)
    s0[...] = total[:rows]
    s12[...] = total[rows : 3 * rows].astype(BF16)
    s3[...] = total[3 * rows :]


def chip_sum(home, other):
    vmem = pl.BlockSpec(memory_space=pltpu.VMEM)
    cols = home.shape[1]
    return pl.pallas_call(
        chip_sum_kernel,
        out_shape=[
            jax.ShapeDtypeStruct((2 * BLK, cols), F32),
            jax.ShapeDtypeStruct((4 * BLK, cols), BF16),
            jax.ShapeDtypeStruct((2 * BLK, cols), F32),
        ],
        in_specs=[vmem] * 2,
        out_specs=[vmem] * 3,
        compiler_params=params(),
        cost_estimate=cost(0.5),
        name="chip_sum",
    )(home, other)


def input_grad_kernel(g0, g1, g3, g2, weight_ref, out_ref):
    grads = jnp.concatenate([g0[...], g1[...], g3[...], g2[...]], axis=0)
    out_ref[...] = dot_nt(grads, weight_ref[...]).astype(BF16)


def input_grad_pieces(grads, weight):
    vmem = pl.BlockSpec(memory_space=pltpu.VMEM)
    return pl.pallas_call(
        input_grad_kernel,
        out_shape=jax.ShapeDtypeStruct((4 * SEG, 2 * PART), BF16),
        in_specs=[vmem] * 5,
        out_specs=vmem,
        compiler_params=params(),
        cost_estimate=cost(0.8),
        name="input_grad_pieces",
    )(*grads, weight)


def shards(fwd_x, fwd_q, bwd_x, bwd_q, bwd_dout, cache_kv, kv_weight, seg_lengths):
    shard = kv_weight[0]
    lengths = seg_lengths[0, 0]
    cache = cache_kv[0, 0]
    front_q, back_q, back_dout = fwd_q[0, 0], bwd_q[0, 0], bwd_dout[0, 0]
    together = lax.optimization_barrier
    rows = functools.partial(jnp.concatenate, axis=0)

    across = swap(shard, z=1)
    split = split_inputs(fwd_x[0, 0], bwd_x[0, 0])
    pieces = [split[0]] + [swap(split[r], x=r) for r in (1, 2, 3)]

    pair = rows([shard, across])
    token, pair, pieces[0] = together((lengths, pair, pieces[0]))
    pair_came = swap(pair, y=1)
    grad_query, kv_grad = backward_groups(token, back_q, back_dout, cache)
    pairs = rows([pair, pair_came])
    token, kv_grad, pairs, *came = together((lengths, kv_grad, pairs, *(pieces[r] for r in (2, 1, 3))))
    pieces = [pieces[0], came[1], came[0], came[2]]
    far_kv, left_kv, right_kv = [swap(kv_grad, x=r) for r in (2, 3, 1)]
    grads = [kv_grad, right_kv, left_kv, far_kv]
    pairs_came = swap(pairs, y=3)
    held_a = stored_groups(token, front_q, cache, 0)
    far_kv, left_kv, right_kv, acc, stat = together((far_kv, left_kv, right_kv, *held_a))
    grads = [kv_grad, right_kv, left_kv, far_kv]
    away, home = weight_grad_halves(pieces, grads)
    other_away = swap(away, c=1)
    half = rows([pairs, pairs_came])
    half, away = together((half, away))
    other_half = swap(half, c=1)
    sum0, sum12, sum3 = chip_sum(home, other_away)
    sum_came = swap(sum12, y=1)
    other_half, sum12 = together((other_half, sum12))
    own0, own1, own2, own3, weight = own_kv_parts(pieces, (half, other_half))
    own_came = [swap(own2, x=2), swap(own1, x=1), swap(own3, x=3)]
    leave = input_grad_pieces(grads, weight)
    here = lax.ppermute(leave, "pipe", [(p + 1, p) for p in range(3)])
    token = together((lengths, leave))[0]
    held_b = stored_groups(token, front_q, cache, 2)
    own_came = together((*own_came, held_b[1]))[:3]
    held = (acc, stat, *held_b)
    own2, own1, own3 = own_came
    fwd_out = own_groups(lengths, front_q, (own0, own1, own2, own3), held)
    sum_came = together((sum_came, fwd_out))[0]
    far_leave = (sum3[BLK:] + sum_came[3 * BLK :].astype(F32)).astype(BF16)
    far_last = swap(far_leave, y=3)
    fwd_out = together((fwd_out, far_leave))[0]
    next_act = lax.ppermute(fwd_out, "pipe", [(p, p + 1) for p in range(3)])
    far_total = sum0[BLK:] + sum_came[BLK : 2 * BLK].astype(F32) + far_last.astype(F32)
    far_total = far_total.astype(BF16)
    far_came = swap(far_total, z=1)
    near_leave = (sum3[:BLK] + sum_came[2 * BLK : 3 * BLK].astype(F32)).astype(BF16)
    near_last = swap(near_leave, y=3)
    here = together((here, far_total))[0]
    blocks = [here[at * SEG : (at + 1) * SEG] for at in (0, 1, 3, 2)]
    came = [swap(blocks[r], x=r) for r in (2, 1, 3)]
    far_came, *came, near_last = together((far_came, *came, near_last))
    weight_grad = sum0[:BLK] + sum_came[:BLK].astype(F32) + near_last.astype(F32)
    weight_grad = weight_grad + far_came.astype(F32)
    prev_grad, next_act = join_pieces(blocks[0], came[1], came[0], came[2], next_act)
    return (next_act[None, None], grad_query[None, None], prev_grad[None, None], weight_grad[None])


def solution(mesh):
    return jax.shard_map(
        shards,
        mesh=mesh,
        in_specs=(
            P("pipe", "dp", None, None),
            P("pipe", "dp", None, None),
            P("pipe", "dp", None, None),
            P("pipe", "dp", None, None),
            P("pipe", "dp", None, None),
            P("pipe", "dp", None, None),
            P("pipe", "dp", None),
            P("pipe", "dp", None),
        ),
        out_specs=(
            P("pipe", "dp", None, None),
            P("pipe", "dp", None, None),
            P("pipe", "dp", None, None),
            P("pipe", "dp", None),
        ),
        check_vma=False,
    )
```
